32 devices in a mesh: groups: 2 (over y), tile: 16 (over z, x, core).
Axes of the slice: x: 2, y: 2, z: 4, core: 2. Of those that a mesh axis runs over, the one named last changes fastest.
Arguments:
- features: bfloat16 [192, 16, 16, 256], P(('groups', 'tile')), parts along dimension 0, may hold values from -6 to 6
- weights: bfloat16 [9, 256, 256], replicated, may hold values from -0.125 to 0.125
- grad_out: bfloat16 [192, 16, 16, 256], P(('groups', 'tile')), parts along dimension 0, may hold values from -6 to 6
- tile_pos: int32 [192], P(('groups', 'tile')), parts along dimension 0, may hold values from -1 to 7, as said below
- neighbours: int32 [192, 8], P(('groups', 'tile')), parts along dimension 0, may hold values from -1 to 15, as said below
Outputs:
- activation: bfloat16 [192, 16, 16, 256], P(('groups', 'tile')), parts along dimension 0
- weight_grad: float32 [18, 256, 256], P('groups'), parts along dimension 0
- input_grad: bfloat16 [192, 16, 16, 256], P(('groups', 'tile')), parts along dimension 0
The draws below stay inside these ranges and needn't reach their ends.
There are 2 independent parts, one for each index of `groups`. The reference program is written for one: setup_inputs(seed, part) draws one part's arguments, and reference() takes and returns one part's arrays. A program takes and returns all parts, laid end to end along the dimension named above; an argument that names none is the same for every part. Nothing has to cross between parts.
Inputs may be any that keep to these rules, and one draw needn't show every extreme that they name: `tile_pos`: each device's 6 slots hold the tissue tiles of its band of 2 x 4 tiles first, in raster order, then empty slots; every device holds 2 or more tissue tiles and at least one device holds 6. A code c names slot c % 6 of the device whose index is the own index plus c // 6 - 1; codes of left and right neighbours name the own device, up and up-diagonal neighbours lie on the own or the preceding device, down and down-diagonal ones on the own or the following device. Neighbours are tissue tiles of the slide's grid and the relation is symmetric; empty slots and missing neighbours have -1.
All inputs are finite; a program needn't handle non-finite values.
Results may differ from the reference program's by a relative error of at most 0.0049.
Values may be sent and summed in bfloat16 or wider, within the bound.
A program may use at most 64 MiB of HBM per device.

```python
import math
import jax
import jax.numpy as jnp
from jax import lax

CH = 256
SIDE = 16
TILE_DEV = 6
BAND = 2
GRID_COLS = 4
TILES = 96


ROW_STEPS = (-1, 1, 0, 0, -1, -1, 1, 1)


COL_STEPS = (0, 0, -1, 1, -1, 1, -1, 1)


def slide_layout(key):
    key = jax.random.fold_in(key, 7)
    band_count = TILES // TILE_DEV
    cell_count = BAND * GRID_COLS
    spread = TILE_DEV - 2
    key_first, key_second, key_full, key_order = jax.random.split(key, 4)
    first_draw = jax.random.randint(key_first, (band_count,), 0, spread + 1)
    second = jax.random.randint(key_second, (band_count,), 0, spread + 1)
    counts = 2 + first_draw * second // spread
    chosen = jax.random.randint(key_full, (), 1, band_count)
    band_ids = jnp.arange(band_count, dtype=jnp.int32)
    counts = jnp.where(band_ids == chosen, TILE_DEV, counts).astype(jnp.int32)
    cell_ids = jnp.arange(cell_count, dtype=jnp.int32)
    ranking = jax.vmap(lambda single: jax.random.permutation(single, cell_count))(jax.random.split(key_order, band_count)).astype(jnp.int32)
    ranking = jnp.where(band_ids[:, None] == chosen, cell_ids[None, :], ranking)
    last_rank = ranking[:, cell_count - 1:cell_count]
    bumped = jnp.where(cell_ids[None, :] == cell_count - 1, 0, jnp.where(ranking < last_rank, ranking + 1, ranking))
    ranking = jnp.where(band_ids[:, None] == chosen - 1, bumped, ranking)
    tissue = ranking < counts[:, None]
    raster_order = jnp.argsort(jnp.where(tissue, 0, cell_count) + cell_ids[None, :], axis=1).astype(jnp.int32)
    slot_ids = jnp.arange(TILE_DEV, dtype=jnp.int32)
    positions = jnp.where(slot_ids[None, :] < counts[:, None], raster_order[:, :TILE_DEV], -1).astype(jnp.int32)
    slot_of = jnp.where(tissue, jnp.cumsum(tissue.astype(jnp.int32), axis=1) - 1, -1)
    tile_rows = positions // GRID_COLS
    tile_cols = positions % GRID_COLS
    row_steps = jnp.array(ROW_STEPS, dtype=jnp.int32)
    col_steps = jnp.array(COL_STEPS, dtype=jnp.int32)
    target_row = tile_rows[:, :, None] + row_steps[None, None, :]
    target_col = tile_cols[:, :, None] + col_steps[None, None, :]
    band_step = jnp.where(target_row < 0, -1, jnp.where(target_row >= BAND, 1, 0))
    target_band = band_ids[:, None, None] + band_step
    inside = (positions[:, :, None] >= 0) & (target_col >= 0) & (target_col < GRID_COLS)
    inside = inside & (target_band >= 0) & (target_band < band_count)
    target_cell = jnp.clip((target_row - band_step * BAND) * GRID_COLS + target_col, 0, cell_count - 1)
    found_slot = slot_of[jnp.clip(target_band, 0, band_count - 1), target_cell]
    inside = inside & (found_slot >= 0)
    link_codes = jnp.where(inside, (band_step + 1) * TILE_DEV + found_slot, -1).astype(jnp.int32)
    return (positions.reshape(TILES), link_codes.reshape(TILES, 8))


def draw_tile_pos(key, part):
    return slide_layout(key)[0]


def draw_neighbours(key, part):
    return slide_layout(key)[1]


def levels(stream_key, dims, cuts, least, top_value):
    factor_of, own = 1.0, jax.random.fold_in(stream_key, 6)
    for position, shards_of in cuts:
        steps = jnp.exp(jax.random.uniform(jax.random.fold_in(own, position), (shards_of,), jnp.float32, least / len(cuts), top_value / len(cuts)))
        factor_of = factor_of * jnp.repeat(steps, dims[position] // shards_of).reshape([-1 if axis == position else 1 for axis in range(len(dims))])
    return factor_of


def bell_draw(key, extent, width, reach, shards=(), kind=jnp.bfloat16):
    drawn = width * jax.random.normal(key, extent, jnp.float32)
    if shards:
        drawn = drawn * levels(key, extent, shards, -0.22, 0.18)
    return jnp.clip(drawn, -reach, reach).astype(kind)


def setup_inputs(seed: int = 0, part: int = 0) -> dict:
    key_list = jax.random.split(jax.random.key(seed), 6)
    part_splits = jax.random.split(jax.random.fold_in(key_list[5], part), 6)
    features = bell_draw(part_splits[0], (TILES, SIDE, SIDE, CH), 1.0, 6.0, ((0, 16),))
    weights = bell_draw(key_list[1], (9, CH, CH), (9 * CH) ** -0.5, 0.125)
    grad_out = bell_draw(part_splits[2], (TILES, SIDE, SIDE, CH), 1.0, 6.0, ((0, 16),))
    tile_pos = draw_tile_pos(jax.random.fold_in(jax.random.fold_in(key_list[5], part), 71), part)
    neighbours = draw_neighbours(jax.random.fold_in(jax.random.fold_in(key_list[5], part), 71), part)
    return dict(features=features, weights=weights, grad_out=grad_out, tile_pos=tile_pos, neighbours=neighbours)


EDGE_PICK = (1, 0, 3, 2, 1, 1, 0, 0)
ROOT_HALF = 0.7071067811865476
INV_ROOT_TAU = 0.3989422804014327

def gelu_value(preact):
    return preact * (0.5 * (1.0 + lax.erf(preact * ROOT_HALF)))

def gelu_slope(preact):
    cumulative = 0.5 * (1.0 + lax.erf(preact * ROOT_HALF))
    density = jnp.exp(-0.5 * preact * preact) * INV_ROOT_TAU
    return cumulative + preact * density

def edge_rims(field_map):
    return jnp.stack([field_map[:, 0], field_map[:, -1], field_map[:, :, 0], field_map[:, :, -1]], axis=1)

def surround(center, gathered):
    upper_row = jnp.concatenate([gathered[:, 4, -1:], gathered[:, 0], gathered[:, 5, :1]], axis=1)
    lower_row = jnp.concatenate([gathered[:, 6, -1:], gathered[:, 1], gathered[:, 7, :1]], axis=1)
    middle = jnp.concatenate([gathered[:, 2][:, :, None], center, gathered[:, 3][:, :, None]], axis=2)
    return jnp.concatenate([upper_row[:, None], middle, lower_row[:, None]], axis=1)

def tap_matrix(extended, flipped):
    side_cells = extended.shape[1] - 2
    pieces = []
    for row_tap in range(3):
        for col_tap in range(3):
            row_start = 2 - row_tap if flipped else row_tap
            col_start = 2 - col_tap if flipped else col_tap
            pieces.append(extended[:, row_start:row_start + side_cells, col_start:col_start + side_cells])
    stacked = jnp.concatenate(pieces, axis=-1)
    return stacked.reshape(-1, stacked.shape[-1])

def band_extend(center, edge_table, link_rows, band_index):
    tile_dev = center.shape[0]
    edge_picks = jnp.array(EDGE_PICK, dtype=jnp.int32)
    linked = link_rows >= 0
    source = (band_index * tile_dev + link_rows - tile_dev) * 4 + edge_picks[None, :]
    clipped = jnp.clip(jnp.where(linked, source, 0), 0, edge_table.shape[0] - 1).astype(jnp.int32)
    gathered = jnp.take(edge_table, clipped.reshape(-1), axis=0).reshape(linked.shape + edge_table.shape[1:])
    gathered = jnp.where(linked[:, :, None, None], gathered, jnp.zeros((), gathered.dtype))
    return surround(center, gathered)

def reference(features, weights, grad_out, tile_pos, neighbours):
    band_count = TILES // TILE_DEV
    tissue = (tile_pos >= 0).astype(jnp.float32)
    weight_mat = weights.reshape(9 * CH, CH)
    flip_mat = jnp.transpose(weights, (0, 2, 1)).reshape(9 * CH, CH)
    table_x = edge_rims(features).reshape(TILES * 4, SIDE, CH)
    band_ids = jnp.arange(band_count, dtype=jnp.int32)

    def forward(band_index):
        first_slot = band_index * TILE_DEV
        center = lax.dynamic_slice_in_dim(features, first_slot, TILE_DEV, 0)
        link_rows = lax.dynamic_slice_in_dim(neighbours, first_slot, TILE_DEV, 0)
        tissue_gate = lax.dynamic_slice_in_dim(tissue, first_slot, TILE_DEV, 0)
        grad_tiles = lax.dynamic_slice_in_dim(grad_out, first_slot, TILE_DEV, 0)
        extended = band_extend(center, table_x, link_rows, band_index)
        preact = jnp.dot(tap_matrix(extended, False), weight_mat, preferred_element_type=jnp.float32)
        preact = preact.reshape(TILE_DEV, SIDE, SIDE, CH)
        gate_cells = tissue_gate[:, None, None, None]
        act_map = (gelu_value(preact) * gate_cells).astype(jnp.bfloat16)
        slope_map = (grad_tiles.astype(jnp.float32) * gelu_slope(preact) * gate_cells).astype(jnp.bfloat16)
        return (act_map, slope_map)
    activation, pre_grad = lax.map(forward, band_ids)
    activation = activation.reshape(TILES, SIDE, SIDE, CH)
    pre_grad = pre_grad.reshape(TILES, SIDE, SIDE, CH)
    table_g = edge_rims(pre_grad).reshape(TILES * 4, SIDE, CH)

    def backward(running, band_index):
        first_slot = band_index * TILE_DEV
        center_x = lax.dynamic_slice_in_dim(features, first_slot, TILE_DEV, 0)
        center_g = lax.dynamic_slice_in_dim(pre_grad, first_slot, TILE_DEV, 0)
        link_rows = lax.dynamic_slice_in_dim(neighbours, first_slot, TILE_DEV, 0)
        tissue_gate = lax.dynamic_slice_in_dim(tissue, first_slot, TILE_DEV, 0)
        ext_x = band_extend(center_x, table_x, link_rows, band_index)
        ext_g = band_extend(center_g, table_g, link_rows, band_index)
        running = running + lax.dot_general(tap_matrix(ext_x, False), center_g.reshape(-1, CH), (((0,), (0,)), ((), ())), preferred_element_type=jnp.float32)
        back_map = jnp.dot(tap_matrix(ext_g, True), flip_mat, preferred_element_type=jnp.float32)
        back_map = back_map.reshape(TILE_DEV, SIDE, SIDE, CH) * tissue_gate[:, None, None, None]
        return (running, back_map.astype(jnp.bfloat16))
    summed, input_grad = lax.scan(backward, jnp.zeros((9 * CH, CH), jnp.float32), band_ids)
    grad_scale = 1.0 / math.sqrt(TILES * SIDE * SIDE)
    weight_grad = (summed * grad_scale).reshape(9, CH, CH)
    return (activation, weight_grad, input_grad.reshape(TILES, SIDE, SIDE, CH))
```

```python
import functools
import math

import jax
import jax.numpy as jnp
from jax import lax
from jax.experimental import pallas as pl
from jax.experimental.pallas import tpu as pltpu
from jax.sharding import PartitionSpec as P

ROOT_HALF = 0.7071067811865476
INV_ROOT_TAU = 0.3989422804014327
FAN = 4
LAG_CORE, LAG_NEAR, LAG_FAN, LAG_FAN_BACK, LAG_NEAR_BACK, LAG_CORE_BACK = (1, 3, 5, 7, 9, 10)
MESH = pl.DeviceIdType.MESH


def shifted(center, left, right, axis):
    cell = lax.broadcasted_iota(jnp.int32, center.shape, axis)
    side = center.shape[axis]
    from_left = pltpu.roll(jnp.where(cell == side - 1, left, center), 1, axis)
    from_right = pltpu.roll(jnp.where(cell == 0, right, center), side - 1, axis)
    return from_left, from_right


def kernel(
    count,
    scale,
    features,
    weights,
    grad_out,
    tile_pos,
    links,
    act,
    grad_sum,
    input_grad,
    ext_x,
    ext_g,
    above_x,
    below_x,
    above_g,
    below_g,
    rows_out,
    pre_grad,
    pre_grad_t,
    weights_t,
    part,
    core_out,
    core_in,
    near_out,
    near_in,
    fan_out,
    fan_in,
    far_out,
    far_in,
    total,
    halo_sems,
    core_sems,
    near_sems,
    fan_sems,
    far_sems,
):
    f32, bf16 = jnp.float32, jnp.bfloat16
    tiles, side, _, channels = features.shape
    cells = side * side
    taps = weights.shape[0]
    zero_row = 2 * tiles
    me = lax.axis_index("tile")
    core = lax.rem(me, 2)
    near = lax.rem(me // 2, 2)
    fan = lax.rem(me // 4, FAN)
    base = me - core - 2 * near - 4 * fan
    core_peer = me + 1 - 2 * core
    near_peer = me + 2 - 4 * near
    far_rounds = far_out.shape[1]

    def fan_slot(step):
        return lax.rem(fan + step + FAN, FAN)

    def fan_peer(step):
        return base + 4 * fan_slot(step) + 2 * near + core

    def far_peer(turn):
        stride = 4 * FAN * 2**turn
        return me + stride - 2 * stride * lax.rem(me // stride, 2)

    def send(source, target, sems, peer):
        return pltpu.make_async_remote_copy(
            src_ref=source,
            dst_ref=target,
            send_sem=sems.at[0],
            recv_sem=sems.at[1],
            device_id={"tile": peer},
            device_id_type=MESH,
        )

    has_prev, has_next = me > 0, me < count - 1
    barrier = pltpu.get_barrier_semaphore()
    peers = [core_peer, near_peer] + [fan_peer(step) for step in range(1, FAN)]
    peers = peers + [far_peer(turn) for turn in range(far_rounds)]
    for peer in peers:
        pl.semaphore_signal(barrier, inc=1, device_id={"tile": peer}, device_id_type=MESH)

    @pl.when(has_prev)
    def _():
        pl.semaphore_signal(barrier, inc=1, device_id={"tile": me - 1}, device_id_type=MESH)

    @pl.when(has_next)
    def _():
        pl.semaphore_signal(barrier, inc=1, device_id={"tile": me + 1}, device_id_type=MESH)

    pl.semaphore_wait(barrier, len(peers) + jnp.where(has_prev, 1, 0) + jnp.where(has_next, 1, 0))

    def halo(turn, above, below):
        down = send(rows_out.at[turn, 0], above.at[pl.ds(0, tiles)], halo_sems.at[turn, 0], me + 1)
        up = send(rows_out.at[turn, 1], below.at[pl.ds(tiles, tiles)], halo_sems.at[turn, 1], me - 1)
        return down, up

    def start_halo(turn, field, above, below):
        last, first = field[:, side - 1], field[:, 0]
        rows_out[turn, 0] = last
        rows_out[turn, 1] = first
        down, up = halo(turn, above, below)

        @pl.when(has_next)
        def _():
            down.start()

        @pl.when(has_prev)
        def _():
            up.start()

        above[tiles : 2 * tiles] = last
        below[0:tiles] = first
        for table in (above, below):
            table[zero_row] = jnp.zeros(table.shape[1:], table.dtype)

    def wait_halo(turn, above, below):
        down, up = halo(turn, above, below)

        @pl.when(has_next)
        def _():
            down.wait_send()
            up.wait_recv()

        @pl.when(has_prev)
        def _():
            up.wait_send()
            down.wait_recv()

    def link_gate(code):
        return jnp.where(code >= 0, 1.0, 0.0).astype(f32)

    def inner_rows(field, tile, put):
        center = field[tile]
        left, right = links[tile, 2], links[tile, 3]
        left_map = field[jnp.where(left >= tiles, left - tiles, tile)].astype(f32) * link_gate(left)
        right_map = field[jnp.where(right >= tiles, right - tiles, tile)].astype(f32) * link_gate(right)
        from_left, from_right = shifted(center.astype(f32), left_map, right_map, 1)
        inner = slice(1, side + 1)
        put(0, inner, from_left.astype(bf16))
        put(1, inner, center)
        put(2, inner, from_right.astype(bf16))

    def border_rows(table, row, tile, first_link, left_link, right_link, base_code, put):
        def pick(link):
            code = links[tile, link]
            return table[jnp.where(code >= base_code, code - base_code, zero_row)]

        center = pick(first_link)
        from_left, from_right = shifted(
            center.astype(f32), pick(left_link).astype(f32), pick(right_link).astype(f32), 0
        )
        put(0, row, from_left.astype(bf16))
        put(1, row, center)
        put(2, row, from_right.astype(bf16))

    def both_borders(above, below, tile, put):
        border_rows(above, 0, tile, 0, 4, 5, 0, put)
        border_rows(below, side + 1, tile, 1, 6, 7, tiles, put)

    start_halo(0, features, above_x, below_x)

    def put_x(tile):
        def put(shift, rows, value):
            ext_x[shift, tile, rows] = value

        return put

    @pl.loop(0, tiles)
    def _(tile):
        inner_rows(features, tile, put_x(tile))

    wait_halo(0, above_x, below_x)

    @pl.loop(0, tiles)
    def _(tile):
        both_borders(above_x, below_x, tile, put_x(tile))

    weight_mat_rows = taps * channels

    @pl.loop(0, tiles)
    def _(tile):
        pieces = [
            ext_x[b, tile, a : a + side].reshape(cells, channels) for a in range(3) for b in range(3)
        ]
        preact = jnp.dot(
            jnp.concatenate(pieces, axis=1),
            weights[...].reshape(weight_mat_rows, channels),
            preferred_element_type=f32,
        )
        gate = jnp.where(tile_pos[tile] >= 0, 1.0, 0.0).astype(f32)
        cumulative = 0.5 * (1.0 + lax.erf(preact * ROOT_HALF))
        density = jnp.exp(-0.5 * preact * preact) * INV_ROOT_TAU
        act[tile] = (preact * cumulative * gate).astype(bf16).reshape(side, side, channels)
        grad = grad_out[tile].reshape(cells, channels).astype(f32)
        slope = grad * (cumulative + preact * density) * gate
        pre_grad[tile] = slope.astype(bf16).reshape(side, side, channels)
        pre_grad_t[tile] = slope.T.astype(bf16)

    start_halo(1, pre_grad, above_g, below_g)

    def core_copy(k):
        return send(core_out.at[k], core_in.at[k], core_sems.at[0, k], core_peer)

    def near_copy(k):
        return send(near_out.at[k], near_in.at[k], near_sems.at[0, k], near_peer)

    def fan_copy(k, step):
        return send(
            fan_out.at[k, step - 1],
            fan_in.at[k, step - 1],
            fan_sems.at[0, k, step - 1],
            fan_peer(step),
        )

    def far_copy(k, turn):
        return send(far_out.at[k, turn], far_in.at[k, turn], far_sems.at[k, turn], far_peer(turn))

    def fan_back(k, step, owner):
        block = total.at[k, core, near, owner]
        return send(block, block, fan_sems.at[1, k, step - 1], fan_peer(step))

    def near_back(k, owner):
        block = total.at[k, core, owner]
        return send(block, block, near_sems.at[1, k], near_peer)

    def core_back(k, owner):
        block = total.at[k, owner]
        return send(block, block, core_sems.at[1, k], core_peer)

    @pl.loop(0, taps + LAG_CORE_BACK)
    def _(step):
        @pl.when(step < taps)
        def _():
            k = step
            rows = ext_x[lax.rem(k, 3), :, pl.ds(k // 3, side)].reshape(tiles * cells, channels)
            lhs = jnp.concatenate([pre_grad_t[tile] for tile in range(tiles)], axis=1)
            term = jnp.dot(lhs, rows, preferred_element_type=f32)
            part[k] = term.T.reshape(part.shape[1:])
            core_out[k] = part[k, 1 - core].astype(bf16)
            core_copy(k).start()
            weights_t[k] = weights[k].astype(f32).T.astype(bf16)

        @pl.when((step >= LAG_CORE) & (step < taps + LAG_CORE))
        def _():
            k = step - LAG_CORE
            core_copy(k).wait_recv()
            part[k, core] = part[k, core] + core_in[k].astype(f32)
            near_out[k] = part[k, core, 1 - near].astype(bf16)
            near_copy(k).start()

        @pl.when((step >= LAG_NEAR) & (step < taps + LAG_NEAR))
        def _():
            k = step - LAG_NEAR
            near_copy(k).wait_recv()
            part[k, core, near] = part[k, core, near] + near_in[k].astype(f32)
            for turn in range(1, FAN):
                fan_out[k, turn - 1] = part[k, core, near, fan_slot(turn)].astype(bf16)
                fan_copy(k, turn).start()

        @pl.when((step >= LAG_FAN) & (step < taps + LAG_FAN))
        def _():
            k = step - LAG_FAN
            sums = part[k, core, near, fan]
            for turn in range(1, FAN):
                fan_copy(k, turn).wait_recv()
                sums = sums + fan_in[k, turn - 1].astype(f32)
            for turn in range(far_rounds):
                far_out[k, turn] = sums.astype(bf16)
                copy = far_copy(k, turn)
                copy.start()
                copy.wait()
                sums = far_out[k, turn].astype(f32) + far_in[k, turn].astype(f32)
            total[k, core, near, fan] = (sums * scale).astype(bf16)
            for turn in range(1, FAN):
                fan_back(k, turn, fan).start()

        @pl.when((step >= LAG_FAN_BACK) & (step < taps + LAG_FAN_BACK))
        def _():
            k = step - LAG_FAN_BACK
            for turn in range(1, FAN):
                fan_back(k, turn, fan_slot(-turn)).wait_recv()
            near_back(k, near).start()

        @pl.when((step >= LAG_NEAR_BACK) & (step < taps + LAG_NEAR_BACK))
        def _():
            k = step - LAG_NEAR_BACK
            near_back(k, 1 - near).wait_recv()
            core_back(k, core).start()

        @pl.when(step >= LAG_CORE_BACK)
        def _():
            k = step - LAG_CORE_BACK
            core_back(k, 1 - core).wait_recv()
            core_copy(k).wait_send()
            near_copy(k).wait_send()
            for turn in range(1, FAN):
                fan_copy(k, turn).wait_send()
                fan_back(k, turn, fan).wait_send()
            near_back(k, near).wait_send()
            core_back(k, core).wait_send()
            grad_sum[k] = total[k].reshape(channels, channels)

        @pl.when(step == taps)
        def _():
            wait_halo(1, above_g, below_g)

        @pl.when((step >= taps) & (step < taps + tiles))
        def _():
            tile = step - taps

            def put(shift, rows, value):
                ext_g[shift, rows] = value

            inner_rows(pre_grad, tile, put)
            both_borders(above_g, below_g, tile, put)
            pieces = [
                ext_g[2 - b, 2 - a : 2 - a + side].reshape(cells, channels)
                for a in range(3)
                for b in range(3)
            ]
            back = jnp.dot(
                jnp.concatenate(pieces, axis=1),
                weights_t[...].reshape(weight_mat_rows, channels),
                preferred_element_type=f32,
            )
            gate = jnp.where(tile_pos[tile] >= 0, 1.0, 0.0).astype(f32)
            input_grad[tile] = (back * gate).astype(bf16).reshape(side, side, channels)


def body(count, features, weights, grad_out, tile_pos, neighbours):
    bf16, f32 = jnp.bfloat16, jnp.float32
    tiles, side, _, channels = features.shape
    taps = weights.shape[0]
    scale = 1.0 / math.sqrt(tiles * count * side * side)
    split = (2, 2, FAN, channels // (4 * FAN), channels)
    far_rounds = int(math.log2(count // (4 * FAN)))
    table = pltpu.VMEM((2 * tiles + 1, side, channels), bf16)
    dma = pltpu.SemaphoreType.DMA
    vmem = pl.BlockSpec(memory_space=pltpu.VMEM)
    smem = pl.BlockSpec(memory_space=pltpu.SMEM)
    flops = 3 * 2 * tiles * side * side * taps * channels * channels
    act, grad_sum, input_grad = pl.pallas_call(
        functools.partial(kernel, count, scale),
        out_shape=(
            jax.ShapeDtypeStruct(features.shape, bf16),
            jax.ShapeDtypeStruct(weights.shape, bf16),
            jax.ShapeDtypeStruct(features.shape, bf16),
        ),
        in_specs=[vmem, vmem, vmem, smem, smem],
        out_specs=(vmem, vmem, vmem),
        scratch_shapes=[
            pltpu.VMEM((3, tiles, side + 2, side, channels), bf16),
            pltpu.VMEM((3, side + 2, side, channels), bf16),
            table,
            table,
            table,
            table,
            pltpu.VMEM((2, 2, tiles, side, channels), bf16),
            pltpu.VMEM(features.shape, bf16),
            pltpu.VMEM((tiles, channels, side * side), bf16),
            pltpu.VMEM(weights.shape, bf16),
            pltpu.VMEM((taps,) + split, f32),
            pltpu.VMEM((taps,) + split[1:], bf16),
            pltpu.VMEM((taps,) + split[1:], bf16),
            pltpu.VMEM((taps,) + split[2:], bf16),
            pltpu.VMEM((taps,) + split[2:], bf16),
            pltpu.VMEM((taps, FAN - 1) + split[3:], bf16),
            pltpu.VMEM((taps, FAN - 1) + split[3:], bf16),
            pltpu.VMEM((taps, far_rounds) + split[3:], bf16),
            pltpu.VMEM((taps, far_rounds) + split[3:], bf16),
            pltpu.VMEM((taps,) + split, bf16),
            dma((2, 2, 2)),
            dma((2, taps, 2)),
            dma((2, taps, 2)),
            dma((2, taps, FAN - 1, 2)),
            dma((taps, far_rounds, 2)),
        ],
        compiler_params=pltpu.CompilerParams(
            collective_id=0, has_side_effects=True, vmem_limit_bytes=48 * 2**20
        ),
        cost_estimate=pl.CostEstimate(flops=flops, bytes_accessed=2**23, transcendentals=0),
        name="tile_conv_step",
    )(features, weights, grad_out, tile_pos, neighbours)
    return act, grad_sum.astype(f32), input_grad


def solution(mesh):
    in_specs = (
        P(("groups", "tile"), None, None, None),
        P(),
        P(("groups", "tile"), None, None, None),
        P(("groups", "tile")),
        P(("groups", "tile"), None),
    )
    out_specs = (
        P(("groups", "tile"), None, None, None),
        P("groups", None, None),
        P(("groups", "tile"), None, None, None),
    )
    return jax.shard_map(
        functools.partial(body, mesh.shape["tile"]),
        mesh=mesh,
        in_specs=in_specs,
        out_specs=out_specs,
        check_vma=False,
    )
```

```python
import functools
import math

import jax
import jax.numpy as jnp
from jax import lax
from jax.experimental import pallas as pl
from jax.experimental.pallas import tpu as pltpu
from jax.sharding import PartitionSpec as P

ROOT_HALF = 0.7071067811865476
INV_ROOT_TAU = 0.3989422804014327
FAN = 4
LAG_CORE, LAG_NEAR, LAG_FAN, LAG_FAN_BACK, LAG_NEAR_BACK, LAG_CORE_BACK = (1, 3, 5, 7, 9, 10)
MESH = pl.DeviceIdType.MESH


def shifted(center, left, right, axis):
    cell = lax.broadcasted_iota(jnp.int32, center.shape, axis)
    side = center.shape[axis]
    from_left = pltpu.roll(jnp.where(cell == side - 1, left, center), 1, axis)
    from_right = pltpu.roll(jnp.where(cell == 0, right, center), side - 1, axis)
    return from_left, from_right


def kernel(
    count,
    scale,
    features_hbm,
    weights_hbm,
    grad_out_hbm,
    tile_pos_hbm,
    links_hbm,
    act_hbm,
    grad_sum_hbm,
    input_grad_hbm,
    features,
    weights,
    grad_out,
    tile_pos,
    links,
    act,
    input_grad,
    ext_x,
    ext_g,
    above_x,
    below_x,
    above_g,
    below_g,
    rows_out,
    pre_grad,
    pre_grad_t,
    weights_t,
    part,
    core_out,
    core_in,
    near_out,
    near_in,
    fan_out,
    fan_in,
    far_out,
    far_in,
    total,
    halo_sems,
    core_sems,
    near_sems,
    fan_sems,
    far_sems,
    load_sems,
    act_sem,
    input_grad_sems,
    grad_sum_sems,
):
    f32, bf16 = jnp.float32, jnp.bfloat16
    tiles, side, _, channels = features.shape
    cells = side * side
    taps = weights.shape[0]
    zero_row = 2 * tiles
    me = lax.axis_index("tile")
    core = lax.rem(me, 2)
    near = lax.rem(me // 2, 2)
    fan = lax.rem(me // 4, FAN)
    base = me - core - 2 * near - 4 * fan
    core_peer = me + 1 - 2 * core
    near_peer = me + 2 - 4 * near
    far_rounds = far_out.shape[1]

    def fan_slot(step):
        return lax.rem(fan + step + FAN, FAN)

    def fan_peer(step):
        return base + 4 * fan_slot(step) + 2 * near + core

    def far_peer(turn):
        stride = 4 * FAN * 2**turn
        return me + stride - 2 * stride * lax.rem(me // stride, 2)

    def send(source, target, sems, peer):
        return pltpu.make_async_remote_copy(
            src_ref=source,
            dst_ref=target,
            send_sem=sems.at[0],
            recv_sem=sems.at[1],
            device_id={"tile": peer},
            device_id_type=MESH,
        )

    pairs = (
        (features_hbm, features),
        (links_hbm, links),
        (weights_hbm, weights),
        (tile_pos_hbm, tile_pos),
        (grad_out_hbm, grad_out),
    )
    loads = [pltpu.make_async_copy(*pair, load_sems.at[at]) for at, pair in enumerate(pairs)]
    for load in loads:
        load.start()

    has_prev, has_next = me > 0, me < count - 1
    barrier = pltpu.get_barrier_semaphore()
    peers = [core_peer, near_peer] + [fan_peer(step) for step in range(1, FAN)]
    peers = peers + [far_peer(turn) for turn in range(far_rounds)]
    for peer in peers:
        pl.semaphore_signal(barrier, inc=1, device_id={"tile": peer}, device_id_type=MESH)

    @pl.when(has_prev)
    def _():
        pl.semaphore_signal(barrier, inc=1, device_id={"tile": me - 1}, device_id_type=MESH)

    @pl.when(has_next)
    def _():
        pl.semaphore_signal(barrier, inc=1, device_id={"tile": me + 1}, device_id_type=MESH)

    pl.semaphore_wait(barrier, len(peers) + jnp.where(has_prev, 1, 0) + jnp.where(has_next, 1, 0))

    def halo(turn, above, below):
        down = send(rows_out.at[turn, 0], above.at[pl.ds(0, tiles)], halo_sems.at[turn, 0], me + 1)
        up = send(rows_out.at[turn, 1], below.at[pl.ds(tiles, tiles)], halo_sems.at[turn, 1], me - 1)
        return down, up

    def start_halo(turn, field, above, below):
        last, first = field[:, side - 1], field[:, 0]
        rows_out[turn, 0] = last
        rows_out[turn, 1] = first
        down, up = halo(turn, above, below)

        @pl.when(has_next)
        def _():
            down.start()

        @pl.when(has_prev)
        def _():
            up.start()

        above[tiles : 2 * tiles] = last
        below[0:tiles] = first
        for table in (above, below):
            table[zero_row] = jnp.zeros(table.shape[1:], table.dtype)

    def wait_halo(turn, above, below):
        down, up = halo(turn, above, below)

        @pl.when(has_next)
        def _():
            down.wait_send()
            up.wait_recv()

        @pl.when(has_prev)
        def _():
            up.wait_send()
            down.wait_recv()

    def link_gate(code):
        return jnp.where(code >= 0, 1.0, 0.0).astype(f32)

    def inner_rows(field, tile, put):
        center = field[tile]
        left, right = links[tile, 2], links[tile, 3]
        left_map = field[jnp.where(left >= tiles, left - tiles, tile)].astype(f32) * link_gate(left)
        right_map = field[jnp.where(right >= tiles, right - tiles, tile)].astype(f32) * link_gate(right)
        from_left, from_right = shifted(center.astype(f32), left_map, right_map, 1)
        inner = slice(1, side + 1)
        put(0, inner, from_left.astype(bf16))
        put(1, inner, center)
        put(2, inner, from_right.astype(bf16))

    def border_rows(table, row, tile, first_link, left_link, right_link, base_code, put):
        def pick(link):
            code = links[tile, link]
            return table[jnp.where(code >= base_code, code - base_code, zero_row)]

        center = pick(first_link)
        from_left, from_right = shifted(
            center.astype(f32), pick(left_link).astype(f32), pick(right_link).astype(f32), 0
        )
        put(0, row, from_left.astype(bf16))
        put(1, row, center)
        put(2, row, from_right.astype(bf16))

    def both_borders(above, below, tile, put):
        border_rows(above, 0, tile, 0, 4, 5, 0, put)
        border_rows(below, side + 1, tile, 1, 6, 7, tiles, put)

    loads[0].wait()
    loads[1].wait()

    start_halo(0, features, above_x, below_x)

    def put_x(tile):
        def put(shift, rows, value):
            ext_x[shift, tile, rows] = value

        return put

    @pl.loop(0, tiles)
    def _(tile):
        inner_rows(features, tile, put_x(tile))

    wait_halo(0, above_x, below_x)

    @pl.loop(0, tiles)
    def _(tile):
        both_borders(above_x, below_x, tile, put_x(tile))

    for load in loads[2:]:
        load.wait()

    weight_mat_rows = taps * channels

    @pl.loop(0, tiles)
    def _(tile):
        pieces = [
            ext_x[b, tile, a : a + side].reshape(cells, channels) for a in range(3) for b in range(3)
        ]
        preact = jnp.dot(
            jnp.concatenate(pieces, axis=1),
            weights[...].reshape(weight_mat_rows, channels),
            preferred_element_type=f32,
        )
        gate = jnp.where(tile_pos[tile] >= 0, 1.0, 0.0).astype(f32)
        cumulative = 0.5 * (1.0 + lax.erf(preact * ROOT_HALF))
        density = jnp.exp(-0.5 * preact * preact) * INV_ROOT_TAU
        act[tile] = (preact * cumulative * gate).astype(bf16).reshape(side, side, channels)
        grad = grad_out[tile].reshape(cells, channels).astype(f32)
        slope = grad * (cumulative + preact * density) * gate
        pre_grad[tile] = slope.astype(bf16).reshape(side, side, channels)
        pre_grad_t[tile] = slope.T.astype(bf16)

    start_halo(1, pre_grad, above_g, below_g)
    act_copy = pltpu.make_async_copy(act, act_hbm, act_sem)
    act_copy.start()

    def input_grad_copy(tile):
        return pltpu.make_async_copy(
            input_grad.at[tile], input_grad_hbm.at[tile], input_grad_sems.at[tile]
        )

    def grad_sum_copy(k):
        return pltpu.make_async_copy(total.at[k], grad_sum_hbm.at[k], grad_sum_sems.at[k])

    def core_copy(k):
        return send(core_out.at[k], core_in.at[k], core_sems.at[0, k], core_peer)

    def near_copy(k):
        return send(near_out.at[k], near_in.at[k], near_sems.at[0, k], near_peer)

    def fan_copy(k, step):
        return send(
            fan_out.at[k, step - 1],
            fan_in.at[k, step - 1],
            fan_sems.at[0, k, step - 1],
            fan_peer(step),
        )

    def far_copy(k, turn):
        return send(far_out.at[k, turn], far_in.at[k, turn], far_sems.at[k, turn], far_peer(turn))

    def fan_back(k, step, owner):
        block = total.at[k, core, near, owner]
        return send(block, block, fan_sems.at[1, k, step - 1], fan_peer(step))

    def near_back(k, owner):
        block = total.at[k, core, owner]
        return send(block, block, near_sems.at[1, k], near_peer)

    def core_back(k, owner):
        block = total.at[k, owner]
        return send(block, block, core_sems.at[1, k], core_peer)

    @pl.loop(0, taps + LAG_CORE_BACK)
    def _(step):
        @pl.when(step < taps)
        def _():
            k = step
            rows = ext_x[lax.rem(k, 3), :, pl.ds(k // 3, side)].reshape(tiles * cells, channels)
            lhs = jnp.concatenate([pre_grad_t[tile] for tile in range(tiles)], axis=1)
            term = jnp.dot(lhs, rows, preferred_element_type=f32)
            part[k] = term.T.reshape(part.shape[1:])
            core_out[k] = part[k, 1 - core].astype(bf16)
            core_copy(k).start()
            weights_t[k] = weights[k].astype(f32).T.astype(bf16)

        @pl.when((step >= LAG_CORE) & (step < taps + LAG_CORE))
        def _():
            k = step - LAG_CORE
            core_copy(k).wait_recv()
            part[k, core] = part[k, core] + core_in[k].astype(f32)
            near_out[k] = part[k, core, 1 - near].astype(bf16)
            near_copy(k).start()

        @pl.when((step >= LAG_NEAR) & (step < taps + LAG_NEAR))
        def _():
            k = step - LAG_NEAR
            near_copy(k).wait_recv()
            part[k, core, near] = part[k, core, near] + near_in[k].astype(f32)
            for turn in range(1, FAN):
                fan_out[k, turn - 1] = part[k, core, near, fan_slot(turn)].astype(bf16)
                fan_copy(k, turn).start()

        @pl.when((step >= LAG_FAN) & (step < taps + LAG_FAN))
        def _():
            k = step - LAG_FAN
            sums = part[k, core, near, fan]
            for turn in range(1, FAN):
                fan_copy(k, turn).wait_recv()
                sums = sums + fan_in[k, turn - 1].astype(f32)
            for turn in range(far_rounds):
                far_out[k, turn] = sums.astype(bf16)
                copy = far_copy(k, turn)
                copy.start()
                copy.wait()
                sums = far_out[k, turn].astype(f32) + far_in[k, turn].astype(f32)
            total[k, core, near, fan] = (sums * scale).astype(bf16)
            for turn in range(1, FAN):
                fan_back(k, turn, fan).start()

        @pl.when((step >= LAG_FAN_BACK) & (step < taps + LAG_FAN_BACK))
        def _():
            k = step - LAG_FAN_BACK
            for turn in range(1, FAN):
                fan_back(k, turn, fan_slot(-turn)).wait_recv()
            near_back(k, near).start()

        @pl.when((step >= LAG_NEAR_BACK) & (step < taps + LAG_NEAR_BACK))
        def _():
            k = step - LAG_NEAR_BACK
            near_back(k, 1 - near).wait_recv()
            core_back(k, core).start()

        @pl.when(step >= LAG_CORE_BACK)
        def _():
            k = step - LAG_CORE_BACK
            core_back(k, 1 - core).wait_recv()
            core_copy(k).wait_send()
            near_copy(k).wait_send()
            for turn in range(1, FAN):
                fan_copy(k, turn).wait_send()
                fan_back(k, turn, fan).wait_send()
            near_back(k, near).wait_send()
            core_back(k, core).wait_send()
            grad_sum_copy(k).start()

        @pl.when(step == taps)
        def _():
            wait_halo(1, above_g, below_g)

        @pl.when((step >= taps) & (step < taps + tiles))
        def _():
            tile = step - taps

            def put(shift, rows, value):
                ext_g[shift, rows] = value

            inner_rows(pre_grad, tile, put)
            both_borders(above_g, below_g, tile, put)
            pieces = [
                ext_g[2 - b, 2 - a : 2 - a + side].reshape(cells, channels)
                for a in range(3)
                for b in range(3)
            ]
            back = jnp.dot(
                jnp.concatenate(pieces, axis=1),
                weights_t[...].reshape(weight_mat_rows, channels),
                preferred_element_type=f32,
            )
            gate = jnp.where(tile_pos[tile] >= 0, 1.0, 0.0).astype(f32)
            input_grad[tile] = (back * gate).astype(bf16).reshape(side, side, channels)
            input_grad_copy(tile).start()

    act_copy.wait()

    @pl.loop(0, tiles)
    def _(tile):
        input_grad_copy(tile).wait()

    @pl.loop(0, taps)
    def _(k):
        grad_sum_copy(k).wait()


def finish(act_in, grad_in, back_in, act_out, grad_out, back_out, narrow, wide, sems):
    taps = narrow.shape[0]
    copies = [
        pltpu.make_async_copy(act_in, act_out, sems.at[0, 0]),
        pltpu.make_async_copy(back_in, back_out, sems.at[0, 1]),
    ]
    parts = [pl.ds(start, taps // 3) for start in range(0, taps, taps // 3)]
    loads = [
        pltpu.make_async_copy(grad_in.at[rows], narrow.at[rows], sems.at[1, at])
        for at, rows in enumerate(parts)
    ]
    stores = [
        pltpu.make_async_copy(wide.at[rows], grad_out.at[rows], sems.at[2, at])
        for at, rows in enumerate(parts)
    ]
    for copy in loads + copies:
        copy.start()
    for rows, load, store in zip(parts, loads, stores):
        load.wait()
        wide[rows] = narrow[rows].astype(jnp.float32).reshape(wide[rows].shape)
        store.start()
    for copy in copies + stores:
        copy.wait()


def body(count, features, weights, grad_out, tile_pos, neighbours):
    bf16, f32 = jnp.bfloat16, jnp.float32
    tiles, side, _, channels = features.shape
    taps = weights.shape[0]
    scale = 1.0 / math.sqrt(tiles * count * side * side)
    split = (2, 2, FAN, channels // (4 * FAN), channels)
    far_rounds = int(math.log2(count // (4 * FAN)))
    table = pltpu.VMEM((2 * tiles + 1, side, channels), bf16)
    dma = pltpu.SemaphoreType.DMA
    hbm = pl.BlockSpec(memory_space=pl.ANY)
    flops = 3 * 2 * tiles * side * side * taps * channels * channels
    act, grad_sum, input_grad = pl.pallas_call(
        functools.partial(kernel, count, scale),
        out_shape=(
            jax.ShapeDtypeStruct(features.shape, bf16),
            jax.ShapeDtypeStruct((taps,) + split, bf16),
            jax.ShapeDtypeStruct(features.shape, bf16),
        ),
        in_specs=[hbm] * 5,
        out_specs=(hbm, hbm, hbm),
        scratch_shapes=[
            pltpu.VMEM(features.shape, bf16),
            pltpu.VMEM(weights.shape, bf16),
            pltpu.VMEM(features.shape, bf16),
            pltpu.SMEM(tile_pos.shape, jnp.int32),
            pltpu.SMEM(neighbours.shape, jnp.int32),
            pltpu.VMEM(features.shape, bf16),
            pltpu.VMEM(features.shape, bf16),
            pltpu.VMEM((3, tiles, side + 2, side, channels), bf16),
            pltpu.VMEM((3, side + 2, side, channels), bf16),
            table,
            table,
            table,
            table,
            pltpu.VMEM((2, 2, tiles, side, channels), bf16),
            pltpu.VMEM(features.shape, bf16),
            pltpu.VMEM((tiles, channels, side * side), bf16),
            pltpu.VMEM(weights.shape, bf16),
            pltpu.VMEM((taps,) + split, f32),
            pltpu.VMEM((taps,) + split[1:], bf16),
            pltpu.VMEM((taps,) + split[1:], bf16),
            pltpu.VMEM((taps,) + split[2:], bf16),
            pltpu.VMEM((taps,) + split[2:], bf16),
            pltpu.VMEM((taps, FAN - 1) + split[3:], bf16),
            pltpu.VMEM((taps, FAN - 1) + split[3:], bf16),
            pltpu.VMEM((taps, far_rounds) + split[3:], bf16),
            pltpu.VMEM((taps, far_rounds) + split[3:], bf16),
            pltpu.VMEM((taps,) + split, bf16),
            dma((2, 2, 2)),
            dma((2, taps, 2)),
            dma((2, taps, 2)),
            dma((2, taps, FAN - 1, 2)),
            dma((taps, far_rounds, 2)),
            dma((5,)),
            dma,
            dma((tiles,)),
            dma((taps,)),
        ],
        compiler_params=pltpu.CompilerParams(
            collective_id=0, has_side_effects=True, vmem_limit_bytes=60 * 2**20
        ),
        cost_estimate=pl.CostEstimate(flops=flops, bytes_accessed=2**23, transcendentals=0),
        name="tile_conv_step",
    )(features, weights, grad_out, tile_pos, neighbours)
    return pl.pallas_call(
        finish,
        out_shape=(
            jax.ShapeDtypeStruct(act.shape, bf16),
            jax.ShapeDtypeStruct(weights.shape, f32),
            jax.ShapeDtypeStruct(act.shape, bf16),
        ),
        in_specs=[hbm] * 3,
        out_specs=(hbm, hbm, hbm),
        scratch_shapes=[
            pltpu.VMEM((taps,) + split, bf16),
            pltpu.VMEM(weights.shape, f32),
            dma((3, 3)),
        ],
        compiler_params=pltpu.CompilerParams(vmem_limit_bytes=60 * 2**20),
        name="write_results",
    )(act, grad_sum, input_grad)


def solution(mesh):
    in_specs = (
        P(("groups", "tile"), None, None, None),
        P(),
        P(("groups", "tile"), None, None, None),
        P(("groups", "tile")),
        P(("groups", "tile"), None),
    )
    out_specs = (
        P(("groups", "tile"), None, None, None),
        P("groups", None, None),
        P(("groups", "tile"), None, None, None),
    )
    return jax.shard_map(
        functools.partial(body, mesh.shape["tile"]),
        mesh=mesh,
        in_specs=in_specs,
        out_specs=out_specs,
        check_vma=False,
    )
```

```python
import functools
import math

import jax
import jax.numpy as jnp
from jax import lax
from jax.experimental import pallas as pl
from jax.experimental.pallas import tpu as pltpu
from jax.sharding import PartitionSpec as P

ROOT_HALF = 0.7071067811865476
INV_ROOT_TAU = 0.3989422804014327
FAN = 4
LAG_CORE, LAG_NEAR, LAG_FAN, LAG_FAN_BACK, LAG_NEAR_BACK, LAG_CORE_BACK = (1, 3, 5, 7, 9, 10)
MESH = pl.DeviceIdType.MESH


def shifted(center, left, right, axis):
    cell = lax.broadcasted_iota(jnp.int32, center.shape, axis)
    side = center.shape[axis]
    from_left = pltpu.roll(jnp.where(cell == side - 1, left, center), 1, axis)
    from_right = pltpu.roll(jnp.where(cell == 0, right, center), side - 1, axis)
    return from_left, from_right


def kernel(
    count,
    scale,
    features_hbm,
    weights_hbm,
    grad_out_hbm,
    tile_pos_hbm,
    links_hbm,
    act,
    total,
    input_grad,
    features,
    weights,
    grad_out,
    tile_pos,
    links,
    ext_x,
    ext_g,
    above_x,
    below_x,
    above_g,
    below_g,
    rows_out,
    pre_grad,
    pre_grad_t,
    weights_t,
    part,
    core_out,
    core_in,
    near_out,
    near_in,
    fan_out,
    fan_in,
    far_out,
    far_in,
    halo_sems,
    core_sems,
    near_sems,
    fan_sems,
    far_sems,
    load_sems,
):
    f32, bf16 = jnp.float32, jnp.bfloat16
    tiles, side, _, channels = features.shape
    cells = side * side
    taps = weights.shape[0]
    zero_row = 2 * tiles
    me = lax.axis_index("tile")
    core = lax.rem(me, 2)
    near = lax.rem(me // 2, 2)
    fan = lax.rem(me // 4, FAN)
    base = me - core - 2 * near - 4 * fan
    core_peer = me + 1 - 2 * core
    near_peer = me + 2 - 4 * near
    far_rounds = far_out.shape[1]

    def fan_slot(step):
        return lax.rem(fan + step + FAN, FAN)

    def fan_peer(step):
        return base + 4 * fan_slot(step) + 2 * near + core

    def far_peer(turn):
        stride = 4 * FAN * 2**turn
        return me + stride - 2 * stride * lax.rem(me // stride, 2)

    def send(source, target, sems, peer):
        return pltpu.make_async_remote_copy(
            src_ref=source,
            dst_ref=target,
            send_sem=sems.at[0],
            recv_sem=sems.at[1],
            device_id={"tile": peer},
            device_id_type=MESH,
        )

    pairs = (
        (features_hbm, features),
        (links_hbm, links),
        (weights_hbm, weights),
        (tile_pos_hbm, tile_pos),
        (grad_out_hbm, grad_out),
    )
    loads = [pltpu.make_async_copy(*pair, load_sems.at[at]) for at, pair in enumerate(pairs)]
    for load in loads:
        load.start()

    has_prev, has_next = me > 0, me < count - 1
    barrier = pltpu.get_barrier_semaphore()
    peers = [core_peer, near_peer] + [fan_peer(step) for step in range(1, FAN)]
    peers = peers + [far_peer(turn) for turn in range(far_rounds)]
    for peer in peers:
        pl.semaphore_signal(barrier, inc=1, device_id={"tile": peer}, device_id_type=MESH)

    @pl.when(has_prev)
    def _():
        pl.semaphore_signal(barrier, inc=1, device_id={"tile": me - 1}, device_id_type=MESH)

    @pl.when(has_next)
    def _():
        pl.semaphore_signal(barrier, inc=1, device_id={"tile": me + 1}, device_id_type=MESH)

    pl.semaphore_wait(barrier, len(peers) + jnp.where(has_prev, 1, 0) + jnp.where(has_next, 1, 0))

    def halo(turn, above, below):
        down = send(rows_out.at[turn, 0], above.at[pl.ds(0, tiles)], halo_sems.at[turn, 0], me + 1)
        up = send(rows_out.at[turn, 1], below.at[pl.ds(tiles, tiles)], halo_sems.at[turn, 1], me - 1)
        return down, up

    def start_halo(turn, field, above, below):
        last, first = field[:, side - 1], field[:, 0]
        rows_out[turn, 0] = last
        rows_out[turn, 1] = first
        down, up = halo(turn, above, below)

        @pl.when(has_next)
        def _():
            down.start()

        @pl.when(has_prev)
        def _():
            up.start()

        above[tiles : 2 * tiles] = last
        below[0:tiles] = first
        for table in (above, below):
            table[zero_row] = jnp.zeros(table.shape[1:], table.dtype)

    def wait_halo(turn, above, below):
        down, up = halo(turn, above, below)

        @pl.when(has_next)
        def _():
            down.wait_send()
            up.wait_recv()

        @pl.when(has_prev)
        def _():
            up.wait_send()
            down.wait_recv()

    def link_gate(code):
        return jnp.where(code >= 0, 1.0, 0.0).astype(f32)

    def inner_rows(field, tile, put):
        center = field[tile]
        left, right = links[tile, 2], links[tile, 3]
        left_map = field[jnp.where(left >= tiles, left - tiles, tile)].astype(f32) * link_gate(left)
        right_map = field[jnp.where(right >= tiles, right - tiles, tile)].astype(f32) * link_gate(right)
        from_left, from_right = shifted(center.astype(f32), left_map, right_map, 1)
        inner = slice(1, side + 1)
        put(0, inner, from_left.astype(bf16))
        put(1, inner, center)
        put(2, inner, from_right.astype(bf16))

    def border_rows(table, row, tile, first_link, left_link, right_link, base_code, put):
        def pick(link):
            code = links[tile, link]
            return table[jnp.where(code >= base_code, code - base_code, zero_row)]

        center = pick(first_link)
        from_left, from_right = shifted(
            center.astype(f32), pick(left_link).astype(f32), pick(right_link).astype(f32), 0
        )
        put(0, row, from_left.astype(bf16))
        put(1, row, center)
        put(2, row, from_right.astype(bf16))

    def both_borders(above, below, tile, put):
        border_rows(above, 0, tile, 0, 4, 5, 0, put)
        border_rows(below, side + 1, tile, 1, 6, 7, tiles, put)

    loads[0].wait()
    loads[1].wait()

    start_halo(0, features, above_x, below_x)

    def put_x(tile):
        def put(shift, rows, value):
            ext_x[shift, tile, rows] = value

        return put

    @pl.loop(0, tiles)
    def _(tile):
        inner_rows(features, tile, put_x(tile))

    wait_halo(0, above_x, below_x)

    @pl.loop(0, tiles)
    def _(tile):
        both_borders(above_x, below_x, tile, put_x(tile))

    for load in loads[2:]:
        load.wait()

    weight_mat_rows = taps * channels

    @pl.loop(0, tiles)
    def _(tile):
        pieces = [
            ext_x[b, tile, a : a + side].reshape(cells, channels) for a in range(3) for b in range(3)
        ]
        preact = jnp.dot(
            jnp.concatenate(pieces, axis=1),
            weights[...].reshape(weight_mat_rows, channels),
            preferred_element_type=f32,
        )
        gate = jnp.where(tile_pos[tile] >= 0, 1.0, 0.0).astype(f32)
        cumulative = 0.5 * (1.0 + lax.erf(preact * ROOT_HALF))
        density = jnp.exp(-0.5 * preact * preact) * INV_ROOT_TAU
        act[tile] = (preact * cumulative * gate).astype(bf16).reshape(side, side, channels)
        grad = grad_out[tile].reshape(cells, channels).astype(f32)
        slope = grad * (cumulative + preact * density) * gate
        pre_grad[tile] = slope.astype(bf16).reshape(side, side, channels)
        pre_grad_t[tile] = slope.T.astype(bf16)

    start_halo(1, pre_grad, above_g, below_g)

    def core_copy(k):
        return send(core_out.at[k], core_in.at[k], core_sems.at[0, k], core_peer)

    def near_copy(k):
        return send(near_out.at[k], near_in.at[k], near_sems.at[0, k], near_peer)

    def fan_copy(k, step):
        return send(
            fan_out.at[k, step - 1],
            fan_in.at[k, step - 1],
            fan_sems.at[0, k, step - 1],
            fan_peer(step),
        )

    def far_copy(k, turn):
        return send(far_out.at[k, turn], far_in.at[k, turn], far_sems.at[k, turn], far_peer(turn))

    def fan_back(k, step, owner):
        block = total.at[k, core, near, owner]
        return send(block, block, fan_sems.at[1, k, step - 1], fan_peer(step))

    def near_back(k, owner):
        block = total.at[k, core, owner]
        return send(block, block, near_sems.at[1, k], near_peer)

    def core_back(k, owner):
        block = total.at[k, owner]
        return send(block, block, core_sems.at[1, k], core_peer)

    @pl.loop(0, taps + LAG_CORE_BACK)
    def _(step):
        @pl.when(step < taps)
        def _():
            k = step
            rows = ext_x[lax.rem(k, 3), :, pl.ds(k // 3, side)].reshape(tiles * cells, channels)
            lhs = jnp.concatenate([pre_grad_t[tile] for tile in range(tiles)], axis=1)
            term = jnp.dot(lhs, rows, preferred_element_type=f32)
            part[k] = term.T.reshape(part.shape[1:])
            core_out[k] = part[k, 1 - core].astype(bf16)
            core_copy(k).start()
            weights_t[k] = weights[k].astype(f32).T.astype(bf16)

        @pl.when((step >= LAG_CORE) & (step < taps + LAG_CORE))
        def _():
            k = step - LAG_CORE
            core_copy(k).wait_recv()
            part[k, core] = part[k, core] + core_in[k].astype(f32)
            near_out[k] = part[k, core, 1 - near].astype(bf16)
            near_copy(k).start()

        @pl.when((step >= LAG_NEAR) & (step < taps + LAG_NEAR))
        def _():
            k = step - LAG_NEAR
            near_copy(k).wait_recv()
            part[k, core, near] = part[k, core, near] + near_in[k].astype(f32)
            for turn in range(1, FAN):
                fan_out[k, turn - 1] = part[k, core, near, fan_slot(turn)].astype(bf16)
                fan_copy(k, turn).start()

        @pl.when((step >= LAG_FAN) & (step < taps + LAG_FAN))
        def _():
            k = step - LAG_FAN
            sums = part[k, core, near, fan]
            for turn in range(1, FAN):
                fan_copy(k, turn).wait_recv()
                sums = sums + fan_in[k, turn - 1].astype(f32)
            for turn in range(far_rounds):
                far_out[k, turn] = sums.astype(bf16)
                copy = far_copy(k, turn)
                copy.start()
                copy.wait()
                sums = far_out[k, turn].astype(f32) + far_in[k, turn].astype(f32)
            total[k, core, near, fan] = (sums * scale).astype(bf16)
            for turn in range(1, FAN):
                fan_back(k, turn, fan).start()

        @pl.when((step >= LAG_FAN_BACK) & (step < taps + LAG_FAN_BACK))
        def _():
            k = step - LAG_FAN_BACK
            for turn in range(1, FAN):
                fan_back(k, turn, fan_slot(-turn)).wait_recv()
            near_back(k, near).start()

        @pl.when((step >= LAG_NEAR_BACK) & (step < taps + LAG_NEAR_BACK))
        def _():
            k = step - LAG_NEAR_BACK
            near_back(k, 1 - near).wait_recv()
            core_back(k, core).start()

        @pl.when(step >= LAG_CORE_BACK)
        def _():
            k = step - LAG_CORE_BACK
            core_back(k, 1 - core).wait_recv()
            core_copy(k).wait_send()
            near_copy(k).wait_send()
            for turn in range(1, FAN):
                fan_copy(k, turn).wait_send()
                fan_back(k, turn, fan).wait_send()
            near_back(k, near).wait_send()
            core_back(k, core).wait_send()

        @pl.when(step == taps)
        def _():
            wait_halo(1, above_g, below_g)

        @pl.when((step >= taps) & (step < taps + tiles))
        def _():
            tile = step - taps

            def put(shift, rows, value):
                ext_g[shift, rows] = value

            inner_rows(pre_grad, tile, put)
            both_borders(above_g, below_g, tile, put)
            pieces = [
                ext_g[2 - b, 2 - a : 2 - a + side].reshape(cells, channels)
                for a in range(3)
                for b in range(3)
            ]
            back = jnp.dot(
                jnp.concatenate(pieces, axis=1),
                weights_t[...].reshape(weight_mat_rows, channels),
                preferred_element_type=f32,
            )
            gate = jnp.where(tile_pos[tile] >= 0, 1.0, 0.0).astype(f32)
            input_grad[tile] = (back * gate).astype(bf16).reshape(side, side, channels)


def finish(act_in, grad_in, back_in, act_out, grad_out, back_out, wide, sems):
    taps = wide.shape[0]
    copies = [
        pltpu.make_async_copy(back_in, back_out, sems.at[0]),
        pltpu.make_async_copy(act_in, act_out, sems.at[1]),
    ]
    for copy in copies:
        copy.start()
    for start in range(0, taps, taps // 3):
        rows = pl.ds(start, taps // 3)
        wide[rows] = grad_in[rows].astype(jnp.float32).reshape(wide[rows].shape)
        copies.append(pltpu.make_async_copy(wide.at[rows], grad_out.at[rows], sems.at[len(copies)]))
        copies[-1].start()
    for copy in copies:
        copy.wait()


def body(count, features, weights, grad_out, tile_pos, neighbours):
    bf16, f32 = jnp.bfloat16, jnp.float32
    tiles, side, _, channels = features.shape
    taps = weights.shape[0]
    scale = 1.0 / math.sqrt(tiles * count * side * side)
    split = (2, 2, FAN, channels // (4 * FAN), channels)
    far_rounds = int(math.log2(count // (4 * FAN)))
    table = pltpu.VMEM((2 * tiles + 1, side, channels), bf16)
    dma = pltpu.SemaphoreType.DMA
    hbm = pl.BlockSpec(memory_space=pl.ANY)
    vmem = pl.BlockSpec(memory_space=pltpu.VMEM)
    flops = 3 * 2 * tiles * side * side * taps * channels * channels
    act, grad_sum, input_grad = pl.pallas_call(
        functools.partial(kernel, count, scale),
        out_shape=(
            pltpu.VMEM(features.shape, bf16),
            pltpu.VMEM((taps,) + split, bf16),
            pltpu.VMEM(features.shape, bf16),
        ),
        in_specs=[hbm] * 5,
        out_specs=(vmem, vmem, vmem),
        scratch_shapes=[
            pltpu.VMEM(features.shape, bf16),
            pltpu.VMEM(weights.shape, bf16),
            pltpu.VMEM(features.shape, bf16),
            pltpu.SMEM(tile_pos.shape, jnp.int32),
            pltpu.SMEM(neighbours.shape, jnp.int32),
            pltpu.VMEM((3, tiles, side + 2, side, channels), bf16),
            pltpu.VMEM((3, side + 2, side, channels), bf16),
            table,
            table,
            table,
            table,
            pltpu.VMEM((2, 2, tiles, side, channels), bf16),
            pltpu.VMEM(features.shape, bf16),
            pltpu.VMEM((tiles, channels, side * side), bf16),
            pltpu.VMEM(weights.shape, bf16),
            pltpu.VMEM((taps,) + split, f32),
            pltpu.VMEM((taps,) + split[1:], bf16),
            pltpu.VMEM((taps,) + split[1:], bf16),
            pltpu.VMEM((taps,) + split[2:], bf16),
            pltpu.VMEM((taps,) + split[2:], bf16),
            pltpu.VMEM((taps, FAN - 1) + split[3:], bf16),
            pltpu.VMEM((taps, FAN - 1) + split[3:], bf16),
            pltpu.VMEM((taps, far_rounds) + split[3:], bf16),
            pltpu.VMEM((taps, far_rounds) + split[3:], bf16),
            dma((2, 2, 2)),
            dma((2, taps, 2)),
            dma((2, taps, 2)),
            dma((2, taps, FAN - 1, 2)),
            dma((taps, far_rounds, 2)),
            dma((5,)),
        ],
        compiler_params=pltpu.CompilerParams(
            collective_id=0, has_side_effects=True, vmem_limit_bytes=60 * 2**20
        ),
        cost_estimate=pl.CostEstimate(flops=flops, bytes_accessed=2**23, transcendentals=0),
        name="tile_conv_step",
    )(features, weights, grad_out, tile_pos, neighbours)
    return pl.pallas_call(
        finish,
        out_shape=(
            jax.ShapeDtypeStruct(act.shape, bf16),
            jax.ShapeDtypeStruct(weights.shape, f32),
            jax.ShapeDtypeStruct(act.shape, bf16),
        ),
        in_specs=[vmem] * 3,
        out_specs=(hbm, hbm, hbm),
        scratch_shapes=[
            pltpu.VMEM(weights.shape, f32),
            dma((5,)),
        ],
        compiler_params=pltpu.CompilerParams(vmem_limit_bytes=8 * 2**20),
        name="write_results",
    )(act, grad_sum, input_grad)


def solution(mesh):
    in_specs = (
        P(("groups", "tile"), None, None, None),
        P(),
        P(("groups", "tile"), None, None, None),
        P(("groups", "tile")),
        P(("groups", "tile"), None),
    )
    out_specs = (
        P(("groups", "tile"), None, None, None),
        P("groups", None, None),
        P(("groups", "tile"), None, None, None),
    )
    return jax.shard_map(
        functools.partial(body, mesh.shape["tile"]),
        mesh=mesh,
        in_specs=in_specs,
        out_specs=out_specs,
        check_vma=False,
    )
```

```python
import functools
import math

import jax
import jax.numpy as jnp
from jax import lax
from jax.experimental import pallas as pl
from jax.experimental.pallas import tpu as pltpu
from jax.sharding import PartitionSpec as P

ROOT_HALF = 0.7071067811865476
INV_ROOT_TAU = 0.3989422804014327
FAN = 4
GROUP = 3
LAG_CORE, LAG_NEAR, LAG_FAN, LAG_FAN_BACK, LAG_NEAR_BACK, LAG_CORE_BACK = (1, 3, 5, 7, 9, 10)
MESH = pl.DeviceIdType.MESH


def shifted(center, left, right, axis):
    cell = lax.broadcasted_iota(jnp.int32, center.shape, axis)
    side = center.shape[axis]
    from_left = pltpu.roll(jnp.where(cell == side - 1, left, center), 1, axis)
    from_right = pltpu.roll(jnp.where(cell == 0, right, center), side - 1, axis)
    return from_left, from_right


def kernel(
    count,
    scale,
    features_hbm,
    weights_hbm,
    grad_out_hbm,
    tile_pos_hbm,
    links_hbm,
    act,
    total,
    input_grad,
    features,
    weights,
    grad_out,
    tile_pos,
    links,
    ext_x,
    ext_g,
    above_x,
    below_x,
    above_g,
    below_g,
    rows_out,
    pre_grad,
    pre_grad_t,
    weights_t,
    part,
    core_out,
    core_in,
    near_out,
    near_in,
    fan_out,
    fan_in,
    far_out,
    far_in,
    halo_sems,
    core_sems,
    near_sems,
    fan_sems,
    far_sems,
    load_sems,
):
    f32, bf16 = jnp.float32, jnp.bfloat16
    tiles, side, _, channels = features.shape
    cells = side * side
    taps = weights.shape[0]
    zero_row = 2 * tiles
    me = lax.axis_index("tile")
    core = lax.rem(me, 2)
    near = lax.rem(me // 2, 2)
    fan = lax.rem(me // 4, FAN)
    base = me - core - 2 * near - 4 * fan
    core_peer = me + 1 - 2 * core
    near_peer = me + 2 - 4 * near
    far_rounds = far_out.shape[1]

    def fan_slot(step):
        return lax.rem(fan + step + FAN, FAN)

    def fan_peer(step):
        return base + 4 * fan_slot(step) + 2 * near + core

    def far_peer(turn):
        stride = 4 * FAN * 2**turn
        return me + stride - 2 * stride * lax.rem(me // stride, 2)

    def send(source, target, sems, peer):
        return pltpu.make_async_remote_copy(
            src_ref=source,
            dst_ref=target,
            send_sem=sems.at[0],
            recv_sem=sems.at[1],
            device_id={"tile": peer},
            device_id_type=MESH,
        )

    pairs = (
        (features_hbm, features),
        (links_hbm, links),
        (weights_hbm, weights),
        (tile_pos_hbm, tile_pos),
        (grad_out_hbm, grad_out),
    )
    loads = [pltpu.make_async_copy(*pair, load_sems.at[at]) for at, pair in enumerate(pairs)]
    for load in loads:
        load.start()

    has_prev, has_next = me > 0, me < count - 1
    barrier = pltpu.get_barrier_semaphore()
    peers = [core_peer, near_peer] + [fan_peer(step) for step in range(1, FAN)]
    peers = peers + [far_peer(turn) for turn in range(far_rounds)]
    for peer in peers:
        pl.semaphore_signal(barrier, inc=1, device_id={"tile": peer}, device_id_type=MESH)

    @pl.when(has_prev)
    def _():
        pl.semaphore_signal(barrier, inc=1, device_id={"tile": me - 1}, device_id_type=MESH)

    @pl.when(has_next)
    def _():
        pl.semaphore_signal(barrier, inc=1, device_id={"tile": me + 1}, device_id_type=MESH)

    pl.semaphore_wait(barrier, len(peers) + jnp.where(has_prev, 1, 0) + jnp.where(has_next, 1, 0))

    def halo(turn, above, below):
        down = send(rows_out.at[turn, 0], above.at[pl.ds(0, tiles)], halo_sems.at[turn, 0], me + 1)
        up = send(rows_out.at[turn, 1], below.at[pl.ds(tiles, tiles)], halo_sems.at[turn, 1], me - 1)
        return down, up

    def start_halo(turn, field, above, below):
        last, first = field[:, side - 1], field[:, 0]
        rows_out[turn, 0] = last
        rows_out[turn, 1] = first
        down, up = halo(turn, above, below)

        @pl.when(has_next)
        def _():
            down.start()

        @pl.when(has_prev)
        def _():
            up.start()

        above[tiles : 2 * tiles] = last
        below[0:tiles] = first
        for table in (above, below):
            table[zero_row] = jnp.zeros(table.shape[1:], table.dtype)

    def wait_halo(turn, above, below):
        down, up = halo(turn, above, below)

        @pl.when(has_next)
        def _():
            down.wait_send()
            up.wait_recv()

        @pl.when(has_prev)
        def _():
            up.wait_send()
            down.wait_recv()

    def link_gate(code):
        return jnp.where(code >= 0, 1.0, 0.0).astype(f32)

    def inner_rows(field, tile, put):
        center = field[tile]
        left, right = links[tile, 2], links[tile, 3]
        left_map = field[jnp.where(left >= tiles, left - tiles, tile)].astype(f32) * link_gate(left)
        right_map = field[jnp.where(right >= tiles, right - tiles, tile)].astype(f32) * link_gate(right)
        from_left, from_right = shifted(center.astype(f32), left_map, right_map, 1)
        inner = slice(1, side + 1)
        put(0, inner, from_left.astype(bf16))
        put(1, inner, center)
        put(2, inner, from_right.astype(bf16))

    def border_rows(table, row, tile, first_link, left_link, right_link, base_code, put):
        def pick(link):
            code = links[tile, link]
            return table[jnp.where(code >= base_code, code - base_code, zero_row)]

        center = pick(first_link)
        from_left, from_right = shifted(
            center.astype(f32), pick(left_link).astype(f32), pick(right_link).astype(f32), 0
        )
        put(0, row, from_left.astype(bf16))
        put(1, row, center)
        put(2, row, from_right.astype(bf16))

    def both_borders(above, below, tile, put):
        border_rows(above, 0, tile, 0, 4, 5, 0, put)
        border_rows(below, side + 1, tile, 1, 6, 7, tiles, put)

    loads[0].wait()
    loads[1].wait()

    start_halo(0, features, above_x, below_x)

    def put_x(tile):
        def put(shift, rows, value):
            ext_x[shift, tile, rows] = value

        return put

    @pl.loop(0, tiles)
    def _(tile):
        inner_rows(features, tile, put_x(tile))

    wait_halo(0, above_x, below_x)

    @pl.loop(0, tiles)
    def _(tile):
        both_borders(above_x, below_x, tile, put_x(tile))

    for load in loads[2:]:
        load.wait()

    weight_mat_rows = taps * channels

    def forward_dot(tile):
        pieces = [
            ext_x[b, tile, a : a + side].reshape(cells, channels) for a in range(3) for b in range(3)
        ]
        return jnp.dot(
            jnp.concatenate(pieces, axis=1),
            weights[...].reshape(weight_mat_rows, channels),
            preferred_element_type=f32,
        )

    def forward_point(tile, preact):
        gate = jnp.where(tile_pos[tile] >= 0, 1.0, 0.0).astype(f32)
        cumulative = 0.5 * (1.0 + lax.erf(preact * ROOT_HALF))
        density = jnp.exp(-0.5 * preact * preact) * INV_ROOT_TAU
        act[tile] = (preact * cumulative * gate).astype(bf16).reshape(side, side, channels)
        grad = grad_out[tile].reshape(cells, channels).astype(f32)
        slope = grad * (cumulative + preact * density) * gate
        pre_grad[tile] = slope.astype(bf16).reshape(side, side, channels)
        pre_grad_t[tile] = slope.T.astype(bf16)

    batch = GROUP if tiles % GROUP == 0 else 1

    @pl.loop(0, tiles // batch)
    def _(turn):
        group = [turn * batch + at for at in range(batch)]
        preacts = [forward_dot(tile) for tile in group]
        for tile, preact in zip(group, preacts):
            forward_point(tile, preact)

    start_halo(1, pre_grad, above_g, below_g)

    def core_copy(k):
        return send(core_out.at[k], core_in.at[k], core_sems.at[0, k], core_peer)

    def near_copy(k):
        return send(near_out.at[k], near_in.at[k], near_sems.at[0, k], near_peer)

    def fan_copy(k, step):
        return send(
            fan_out.at[k, step - 1],
            fan_in.at[k, step - 1],
            fan_sems.at[0, k, step - 1],
            fan_peer(step),
        )

    def far_copy(k, turn):
        return send(far_out.at[k, turn], far_in.at[k, turn], far_sems.at[k, turn], far_peer(turn))

    def fan_back(k, step, owner):
        block = total.at[k, core, near, owner]
        return send(block, block, fan_sems.at[1, k, step - 1], fan_peer(step))

    def near_back(k, owner):
        block = total.at[k, core, owner]
        return send(block, block, near_sems.at[1, k], near_peer)

    def core_back(k, owner):
        block = total.at[k, owner]
        return send(block, block, core_sems.at[1, k], core_peer)

    def put_g(tile):
        def put(shift, rows, value):
            ext_g[shift, tile, rows] = value

        return put

    @pl.loop(0, taps + LAG_CORE_BACK)
    def _(step):
        @pl.when(step < taps)
        def _():
            k = step
            rows = ext_x[lax.rem(k, 3), :, pl.ds(k // 3, side)].reshape(tiles * cells, channels)
            lhs = jnp.concatenate([pre_grad_t[tile] for tile in range(tiles)], axis=1)
            term = jnp.dot(lhs, rows, preferred_element_type=f32)
            part[k] = term.T.reshape(part.shape[1:])
            core_out[k] = part[k, 1 - core].astype(bf16)
            core_copy(k).start()
            weights_t[k] = weights[k].astype(f32).T.astype(bf16)
            own = jnp.minimum(k, tiles - 1)
            inner_rows(pre_grad, own, put_g(own))

        @pl.when((step >= LAG_CORE) & (step < taps + LAG_CORE))
        def _():
            k = step - LAG_CORE
            core_copy(k).wait_recv()
            part[k, core] = part[k, core] + core_in[k].astype(f32)
            near_out[k] = part[k, core, 1 - near].astype(bf16)
            near_copy(k).start()

        @pl.when((step >= LAG_NEAR) & (step < taps + LAG_NEAR))
        def _():
            k = step - LAG_NEAR
            near_copy(k).wait_recv()
            part[k, core, near] = part[k, core, near] + near_in[k].astype(f32)
            for turn in range(1, FAN):
                fan_out[k, turn - 1] = part[k, core, near, fan_slot(turn)].astype(bf16)
                fan_copy(k, turn).start()

        @pl.when((step >= LAG_FAN) & (step < taps + LAG_FAN))
        def _():
            k = step - LAG_FAN
            sums = part[k, core, near, fan]
            for turn in range(1, FAN):
                fan_copy(k, turn).wait_recv()
                sums = sums + fan_in[k, turn - 1].astype(f32)
            for turn in range(far_rounds):
                far_out[k, turn] = sums.astype(bf16)
                copy = far_copy(k, turn)
                copy.start()
                copy.wait()
                sums = far_out[k, turn].astype(f32) + far_in[k, turn].astype(f32)
            total[k, core, near, fan] = (sums * scale).astype(bf16)
            for turn in range(1, FAN):
                fan_back(k, turn, fan).start()

        @pl.when((step >= LAG_FAN_BACK) & (step < taps + LAG_FAN_BACK))
        def _():
            k = step - LAG_FAN_BACK
            for turn in range(1, FAN):
                fan_back(k, turn, fan_slot(-turn)).wait_recv()
            near_back(k, near).start()

        @pl.when((step >= LAG_NEAR_BACK) & (step < taps + LAG_NEAR_BACK))
        def _():
            k = step - LAG_NEAR_BACK
            near_back(k, 1 - near).wait_recv()
            core_back(k, core).start()

        @pl.when(step >= LAG_CORE_BACK)
        def _():
            k = step - LAG_CORE_BACK
            core_back(k, 1 - core).wait_recv()
            core_copy(k).wait_send()
            near_copy(k).wait_send()
            for turn in range(1, FAN):
                fan_copy(k, turn).wait_send()
                fan_back(k, turn, fan).wait_send()
            near_back(k, near).wait_send()
            core_back(k, core).wait_send()

        @pl.when(step == taps - 1)
        def _():
            wait_halo(1, above_g, below_g)

            @pl.loop(0, tiles)
            def _(tile):
                both_borders(above_g, below_g, tile, put_g(tile))

        @pl.when((step >= taps) & (step < taps + tiles))
        def _():
            tile = step - taps
            pieces = [
                ext_g[2 - b, tile, 2 - a : 2 - a + side].reshape(cells, channels)
                for a in range(3)
                for b in range(3)
            ]
            back = jnp.dot(
                jnp.concatenate(pieces, axis=1),
                weights_t[...].reshape(weight_mat_rows, channels),
                preferred_element_type=f32,
            )
            gate = jnp.where(tile_pos[tile] >= 0, 1.0, 0.0).astype(f32)
            input_grad[tile] = (back * gate).astype(bf16).reshape(side, side, channels)


def finish(act_in, grad_in, back_in, act_out, grad_out, back_out, wide, sems):
    taps = wide.shape[0]
    copies = [
        pltpu.make_async_copy(back_in, back_out, sems.at[0]),
        pltpu.make_async_copy(act_in, act_out, sems.at[1]),
    ]
    for copy in copies:
        copy.start()
    for start in range(0, taps, taps // 3):
        rows = pl.ds(start, taps // 3)
        wide[rows] = grad_in[rows].astype(jnp.float32).reshape(wide[rows].shape)
        copies.append(pltpu.make_async_copy(wide.at[rows], grad_out.at[rows], sems.at[len(copies)]))
        copies[-1].start()
    for copy in copies:
        copy.wait()


def body(count, features, weights, grad_out, tile_pos, neighbours):
    bf16, f32 = jnp.bfloat16, jnp.float32
    tiles, side, _, channels = features.shape
    taps = weights.shape[0]
    scale = 1.0 / math.sqrt(tiles * count * side * side)
    split = (2, 2, FAN, channels // (4 * FAN), channels)
    far_rounds = int(math.log2(count // (4 * FAN)))
    table = pltpu.VMEM((2 * tiles + 1, side, channels), bf16)
    dma = pltpu.SemaphoreType.DMA
    hbm = pl.BlockSpec(memory_space=pl.ANY)
    vmem = pl.BlockSpec(memory_space=pltpu.VMEM)
    flops = 3 * 2 * tiles * side * side * taps * channels * channels
    act, grad_sum, input_grad = pl.pallas_call(
        functools.partial(kernel, count, scale),
        out_shape=(
            pltpu.VMEM(features.shape, bf16),
            pltpu.VMEM((taps,) + split, bf16),
            pltpu.VMEM(features.shape, bf16),
        ),
        in_specs=[hbm] * 5,
        out_specs=(vmem, vmem, vmem),
        scratch_shapes=[
            pltpu.VMEM(features.shape, bf16),
            pltpu.VMEM(weights.shape, bf16),
            pltpu.VMEM(features.shape, bf16),
            pltpu.SMEM(tile_pos.shape, jnp.int32),
            pltpu.SMEM(neighbours.shape, jnp.int32),
            pltpu.VMEM((3, tiles, side + 2, side, channels), bf16),
            pltpu.VMEM((3, tiles, side + 2, side, channels), bf16),
            table,
            table,
            table,
            table,
            pltpu.VMEM((2, 2, tiles, side, channels), bf16),
            pltpu.VMEM(features.shape, bf16),
            pltpu.VMEM((tiles, channels, side * side), bf16),
            pltpu.VMEM(weights.shape, bf16),
            pltpu.VMEM((taps,) + split, f32),
            pltpu.VMEM((taps,) + split[1:], bf16),
            pltpu.VMEM((taps,) + split[1:], bf16),
            pltpu.VMEM((taps,) + split[2:], bf16),
            pltpu.VMEM((taps,) + split[2:], bf16),
            pltpu.VMEM((taps, FAN - 1) + split[3:], bf16),
            pltpu.VMEM((taps, FAN - 1) + split[3:], bf16),
            pltpu.VMEM((taps, far_rounds) + split[3:], bf16),
            pltpu.VMEM((taps, far_rounds) + split[3:], bf16),
            dma((2, 2, 2)),
            dma((2, taps, 2)),
            dma((2, taps, 2)),
            dma((2, taps, FAN - 1, 2)),
            dma((taps, far_rounds, 2)),
            dma((5,)),
        ],
        compiler_params=pltpu.CompilerParams(
            collective_id=0, has_side_effects=True, vmem_limit_bytes=60 * 2**20
        ),
        cost_estimate=pl.CostEstimate(flops=flops, bytes_accessed=2**23, transcendentals=0),
        name="tile_conv_step",
    )(features, weights, grad_out, tile_pos, neighbours)
    return pl.pallas_call(
        finish,
        out_shape=(
            jax.ShapeDtypeStruct(act.shape, bf16),
            jax.ShapeDtypeStruct(weights.shape, f32),
            jax.ShapeDtypeStruct(act.shape, bf16),
        ),
        in_specs=[vmem] * 3,
        out_specs=(hbm, hbm, hbm),
        scratch_shapes=[
            pltpu.VMEM(weights.shape, f32),
            dma((5,)),
        ],
        compiler_params=pltpu.CompilerParams(vmem_limit_bytes=8 * 2**20),
        name="write_results",
    )(act, grad_sum, input_grad)


def solution(mesh):
    in_specs = (
        P(("groups", "tile"), None, None, None),
        P(),
        P(("groups", "tile"), None, None, None),
        P(("groups", "tile")),
        P(("groups", "tile"), None),
    )
    out_specs = (
        P(("groups", "tile"), None, None, None),
        P("groups", None, None),
        P(("groups", "tile"), None, None, None),
    )
    return jax.shard_map(
        functools.partial(body, mesh.shape["tile"]),
        mesh=mesh,
        in_specs=in_specs,
        out_specs=out_specs,
        check_vma=False,
    )
```

```python
import functools
import math

import jax
import jax.numpy as jnp
from jax import lax
from jax.experimental import pallas as pl
from jax.experimental.pallas import tpu as pltpu
from jax.sharding import PartitionSpec as P

ROOT_HALF = 0.7071067811865476
INV_ROOT_TAU = 0.3989422804014327
FAN = 4
GROUP = 3
CHUNK = 3
LAG_CORE, LAG_NEAR, LAG_FAN, LAG_FAN_BACK, LAG_NEAR_BACK, LAG_CORE_BACK = (1, 3, 6, 9, 12, 14)
MESH = pl.DeviceIdType.MESH


def shifted(center, left, right, axis):
    cell = lax.broadcasted_iota(jnp.int32, center.shape, axis)
    side = center.shape[axis]
    from_left = pltpu.roll(jnp.where(cell == side - 1, left, center), 1, axis)
    from_right = pltpu.roll(jnp.where(cell == 0, right, center), side - 1, axis)
    return from_left, from_right


def kernel(
    count,
    scale,
    features_hbm,
    weights_hbm,
    grad_out_hbm,
    tile_pos_hbm,
    links_hbm,
    act,
    total,
    input_grad,
    features,
    weights,
    grad_out,
    tile_pos,
    links,
    ext_x,
    ext_g,
    above_x,
    below_x,
    above_g,
    below_g,
    rows_out,
    pre_grad,
    pre_grad_t,
    weights_t,
    part,
    core_out,
    core_in,
    near_out,
    near_in,
    fan_out,
    fan_in,
    far_out,
    far_in,
    halo_sems,
    core_sems,
    near_sems,
    fan_sems,
    far_sems,
    load_sems,
):
    f32, bf16 = jnp.float32, jnp.bfloat16
    tiles, side, _, channels = features.shape
    cells = side * side
    taps = weights.shape[0]
    zero_row = 2 * tiles
    me = lax.axis_index("tile")
    core = lax.rem(me, 2)
    near = lax.rem(me // 2, 2)
    fan = lax.rem(me // 4, FAN)
    base = me - core - 2 * near - 4 * fan
    core_peer = me + 1 - 2 * core
    near_peer = me + 2 - 4 * near
    far_rounds = far_out.shape[1]

    def fan_slot(step):
        return lax.rem(fan + step + FAN, FAN)

    def fan_peer(step):
        return base + 4 * fan_slot(step) + 2 * near + core

    def far_peer(turn):
        stride = 4 * FAN * 2**turn
        return me + stride - 2 * stride * lax.rem(me // stride, 2)

    def send(source, target, sems, peer):
        return pltpu.make_async_remote_copy(
            src_ref=source,
            dst_ref=target,
            send_sem=sems.at[0],
            recv_sem=sems.at[1],
            device_id={"tile": peer},
            device_id_type=MESH,
        )

    pairs = (
        (features_hbm, features),
        (links_hbm, links),
        (weights_hbm, weights),
        (tile_pos_hbm, tile_pos),
        (grad_out_hbm, grad_out),
    )
    loads = [pltpu.make_async_copy(*pair, load_sems.at[at]) for at, pair in enumerate(pairs)]
    for load in loads:
        load.start()

    has_prev, has_next = me > 0, me < count - 1
    barrier = pltpu.get_barrier_semaphore()
    peers = [core_peer, near_peer] + [fan_peer(step) for step in range(1, FAN)]
    peers = peers + [far_peer(turn) for turn in range(far_rounds)]
    for peer in peers:
        pl.semaphore_signal(barrier, inc=1, device_id={"tile": peer}, device_id_type=MESH)

    @pl.when(has_prev)
    def _():
        pl.semaphore_signal(barrier, inc=1, device_id={"tile": me - 1}, device_id_type=MESH)

    @pl.when(has_next)
    def _():
        pl.semaphore_signal(barrier, inc=1, device_id={"tile": me + 1}, device_id_type=MESH)

    pl.semaphore_wait(barrier, len(peers) + jnp.where(has_prev, 1, 0) + jnp.where(has_next, 1, 0))

    def halo(turn, above, below):
        down = send(rows_out.at[turn, 0], above.at[pl.ds(0, tiles)], halo_sems.at[turn, 0], me + 1)
        up = send(rows_out.at[turn, 1], below.at[pl.ds(tiles, tiles)], halo_sems.at[turn, 1], me - 1)
        return down, up

    def start_halo(turn, field, above, below):
        last, first = field[:, side - 1], field[:, 0]
        rows_out[turn, 0] = last
        rows_out[turn, 1] = first
        down, up = halo(turn, above, below)

        @pl.when(has_next)
        def _():
            down.start()

        @pl.when(has_prev)
        def _():
            up.start()

        above[tiles : 2 * tiles] = last
        below[0:tiles] = first
        for table in (above, below):
            table[zero_row] = jnp.zeros(table.shape[1:], table.dtype)

    def wait_halo(turn, above, below):
        down, up = halo(turn, above, below)

        @pl.when(has_next)
        def _():
            down.wait_send()
            up.wait_recv()

        @pl.when(has_prev)
        def _():
            up.wait_send()
            down.wait_recv()

    def link_gate(code):
        return jnp.where(code >= 0, 1.0, 0.0).astype(f32)

    def inner_rows(field, tile, put):
        center = field[tile]
        left, right = links[tile, 2], links[tile, 3]
        left_map = field[jnp.where(left >= tiles, left - tiles, tile)].astype(f32) * link_gate(left)
        right_map = field[jnp.where(right >= tiles, right - tiles, tile)].astype(f32) * link_gate(right)
        from_left, from_right = shifted(center.astype(f32), left_map, right_map, 1)
        inner = slice(1, side + 1)
        put(0, inner, from_left.astype(bf16))
        put(1, inner, center)
        put(2, inner, from_right.astype(bf16))

    def border_rows(table, row, tile, first_link, left_link, right_link, base_code, put):
        def pick(link):
            code = links[tile, link]
            return table[jnp.where(code >= base_code, code - base_code, zero_row)]

        center = pick(first_link)
        from_left, from_right = shifted(
            center.astype(f32), pick(left_link).astype(f32), pick(right_link).astype(f32), 0
        )
        put(0, row, from_left.astype(bf16))
        put(1, row, center)
        put(2, row, from_right.astype(bf16))

    def both_borders(above, below, tile, put):
        border_rows(above, 0, tile, 0, 4, 5, 0, put)
        border_rows(below, side + 1, tile, 1, 6, 7, tiles, put)

    loads[0].wait()
    loads[1].wait()

    start_halo(0, features, above_x, below_x)

    def put_x(tile):
        def put(shift, rows, value):
            ext_x[shift, tile, rows] = value

        return put

    @pl.loop(0, tiles)
    def _(tile):
        inner_rows(features, tile, put_x(tile))

    wait_halo(0, above_x, below_x)

    @pl.loop(0, tiles)
    def _(tile):
        both_borders(above_x, below_x, tile, put_x(tile))

    for load in loads[2:]:
        load.wait()

    weight_mat_rows = taps * channels

    def forward_dot(tile):
        pieces = [
            ext_x[b, tile, a : a + side].reshape(cells, channels) for a in range(3) for b in range(3)
        ]
        return jnp.dot(
            jnp.concatenate(pieces, axis=1),
            weights[...].reshape(weight_mat_rows, channels),
            preferred_element_type=f32,
        )

    def forward_point(tile, preact):
        gate = jnp.where(tile_pos[tile] >= 0, 1.0, 0.0).astype(f32)
        cumulative = 0.5 * (1.0 + lax.erf(preact * ROOT_HALF))
        density = jnp.exp(-0.5 * preact * preact) * INV_ROOT_TAU
        act[tile] = (preact * cumulative * gate).astype(bf16).reshape(side, side, channels)
        grad = grad_out[tile].reshape(cells, channels).astype(f32)
        slope = grad * (cumulative + preact * density) * gate
        pre_grad[tile] = slope.astype(bf16).reshape(side, side, channels)
        pre_grad_t[tile] = slope.T.astype(bf16)

    batch = GROUP if tiles % GROUP == 0 else 1

    @pl.loop(0, tiles // batch)
    def _(turn):
        group = [turn * batch + at for at in range(batch)]
        preacts = [forward_dot(tile) for tile in group]
        for tile, preact in zip(group, preacts):
            forward_point(tile, preact)

    start_halo(1, pre_grad, above_g, below_g)

    def core_copy(k):
        return send(core_out.at[k], core_in.at[k], core_sems.at[0, k], core_peer)

    def near_copy(k):
        return send(near_out.at[k], near_in.at[k], near_sems.at[0, k], near_peer)

    def fan_copy(k, step):
        return send(
            fan_out.at[k, step - 1],
            fan_in.at[k, step - 1],
            fan_sems.at[0, k, step - 1],
            fan_peer(step),
        )

    def far_copy(k, turn):
        return send(far_out.at[k, turn], far_in.at[k, turn], far_sems.at[k, turn], far_peer(turn))

    def fan_back(k, step, owner):
        block = total.at[k, core, near, owner]
        return send(block, block, fan_sems.at[1, k, step - 1], fan_peer(step))

    def near_back(k, owner):
        block = total.at[k, core, owner]
        return send(block, block, near_sems.at[1, k], near_peer)

    def core_back(k, owner):
        block = total.at[k, owner]
        return send(block, block, core_sems.at[1, k], core_peer)

    def put_g(tile):
        def put(shift, rows, value):
            ext_g[shift, tile, rows] = value

        return put

    chunks = part.shape[0]
    width = taps // chunks

    def due(step, lag):
        since = step - lag - (width - 1)
        return (since >= 0) & (since < taps) & (lax.rem(since, width) == 0)

    def chunk_of(step, lag):
        return (step - lag - (width - 1)) // width

    @pl.loop(0, taps + LAG_CORE_BACK)
    def _(step):
        @pl.when(step < taps)
        def _():
            k = step
            rows = ext_x[lax.rem(k, 3), :, pl.ds(k // 3, side)].reshape(tiles * cells, channels)
            lhs = jnp.concatenate([pre_grad_t[tile] for tile in range(tiles)], axis=1)
            term = jnp.dot(lhs, rows, preferred_element_type=f32)
            chunk, at = k // width, lax.rem(k, width)
            part[chunk, :, :, :, at] = term.T.reshape(part.shape[1:4] + part.shape[5:])
            core_out[chunk, :, :, at] = part[chunk, 1 - core, :, :, at].astype(bf16)

            @pl.when(at == width - 1)
            def _():
                core_copy(chunk).start()

            weights_t[k] = weights[k].astype(f32).T.astype(bf16)
            own = jnp.minimum(k, tiles - 1)
            inner_rows(pre_grad, own, put_g(own))

        @pl.when(due(step, LAG_CORE))
        def _():
            k = chunk_of(step, LAG_CORE)
            core_copy(k).wait_recv()
            part[k, core] = part[k, core] + core_in[k].astype(f32)
            near_out[k] = part[k, core, 1 - near].astype(bf16)
            near_copy(k).start()

        @pl.when(due(step, LAG_NEAR))
        def _():
            k = chunk_of(step, LAG_NEAR)
            near_copy(k).wait_recv()
            part[k, core, near] = part[k, core, near] + near_in[k].astype(f32)
            for turn in range(1, FAN):
                fan_out[k, turn - 1] = part[k, core, near, fan_slot(turn)].astype(bf16)
                fan_copy(k, turn).start()

        @pl.when(due(step, LAG_FAN))
        def _():
            k = chunk_of(step, LAG_FAN)
            sums = part[k, core, near, fan]
            for turn in range(1, FAN):
                fan_copy(k, turn).wait_recv()
                sums = sums + fan_in[k, turn - 1].astype(f32)
            for turn in range(far_rounds):
                far_out[k, turn] = sums.astype(bf16)
                copy = far_copy(k, turn)
                copy.start()
                copy.wait()
                sums = far_out[k, turn].astype(f32) + far_in[k, turn].astype(f32)
            total[k, core, near, fan] = (sums * scale).astype(bf16)
            for turn in range(1, FAN):
                fan_back(k, turn, fan).start()

        @pl.when(due(step, LAG_FAN_BACK))
        def _():
            k = chunk_of(step, LAG_FAN_BACK)
            for turn in range(1, FAN):
                fan_back(k, turn, fan_slot(-turn)).wait_recv()
            near_back(k, near).start()

        @pl.when(due(step, LAG_NEAR_BACK))
        def _():
            k = chunk_of(step, LAG_NEAR_BACK)
            near_back(k, 1 - near).wait_recv()
            core_back(k, core).start()

        @pl.when(due(step, LAG_CORE_BACK))
        def _():
            k = chunk_of(step, LAG_CORE_BACK)
            core_back(k, 1 - core).wait_recv()
            core_copy(k).wait_send()
            near_copy(k).wait_send()
            for turn in range(1, FAN):
                fan_copy(k, turn).wait_send()
                fan_back(k, turn, fan).wait_send()
            near_back(k, near).wait_send()
            core_back(k, core).wait_send()

        @pl.when(step == taps - 1)
        def _():
            wait_halo(1, above_g, below_g)

            @pl.loop(0, tiles)
            def _(tile):
                both_borders(above_g, below_g, tile, put_g(tile))

        @pl.when((step >= taps) & (step < taps + tiles))
        def _():
            tile = step - taps
            pieces = [
                ext_g[2 - b, tile, 2 - a : 2 - a + side].reshape(cells, channels)
                for a in range(3)
                for b in range(3)
            ]
            back = jnp.dot(
                jnp.concatenate(pieces, axis=1),
                weights_t[...].reshape(weight_mat_rows, channels),
                preferred_element_type=f32,
            )
            gate = jnp.where(tile_pos[tile] >= 0, 1.0, 0.0).astype(f32)
            input_grad[tile] = (back * gate).astype(bf16).reshape(side, side, channels)


def finish(act_in, grad_in, back_in, act_out, grad_out, back_out, wide, sems):
    taps = wide.shape[0]
    copies = [
        pltpu.make_async_copy(back_in, back_out, sems.at[0]),
        pltpu.make_async_copy(act_in, act_out, sems.at[1]),
    ]
    for copy in copies:
        copy.start()
    chunks, width = grad_in.shape[0], grad_in.shape[4]
    for chunk in range(chunks):
        for at in range(width):
            block = grad_in[chunk, :, :, :, at].astype(jnp.float32)
            wide[chunk * width + at] = block.reshape(wide.shape[1:])
        rows = pl.ds(chunk * width, width)
        copies.append(pltpu.make_async_copy(wide.at[rows], grad_out.at[rows], sems.at[len(copies)]))
        copies[-1].start()
    for copy in copies:
        copy.wait()


def body(count, features, weights, grad_out, tile_pos, neighbours):
    bf16, f32 = jnp.bfloat16, jnp.float32
    tiles, side, _, channels = features.shape
    taps = weights.shape[0]
    scale = 1.0 / math.sqrt(tiles * count * side * side)
    chunks = taps // CHUNK
    split = (2, 2, FAN, CHUNK, channels // (4 * FAN), channels)
    far_rounds = int(math.log2(count // (4 * FAN)))
    table = pltpu.VMEM((2 * tiles + 1, side, channels), bf16)
    dma = pltpu.SemaphoreType.DMA
    hbm = pl.BlockSpec(memory_space=pl.ANY)
    vmem = pl.BlockSpec(memory_space=pltpu.VMEM)
    flops = 3 * 2 * tiles * side * side * taps * channels * channels
    act, grad_sum, input_grad = pl.pallas_call(
        functools.partial(kernel, count, scale),
        out_shape=(
            pltpu.VMEM(features.shape, bf16),
            pltpu.VMEM((chunks,) + split, bf16),
            pltpu.VMEM(features.shape, bf16),
        ),
        in_specs=[hbm] * 5,
        out_specs=(vmem, vmem, vmem),
        scratch_shapes=[
            pltpu.VMEM(features.shape, bf16),
            pltpu.VMEM(weights.shape, bf16),
            pltpu.VMEM(features.shape, bf16),
            pltpu.SMEM(tile_pos.shape, jnp.int32),
            pltpu.SMEM(neighbours.shape, jnp.int32),
            pltpu.VMEM((3, tiles, side + 2, side, channels), bf16),
            pltpu.VMEM((3, tiles, side + 2, side, channels), bf16),
            table,
            table,
            table,
            table,
            pltpu.VMEM((2, 2, tiles, side, channels), bf16),
            pltpu.VMEM(features.shape, bf16),
            pltpu.VMEM((tiles, channels, side * side), bf16),
            pltpu.VMEM(weights.shape, bf16),
            pltpu.VMEM((chunks,) + split, f32),
            pltpu.VMEM((chunks,) + split[1:], bf16),
            pltpu.VMEM((chunks,) + split[1:], bf16),
            pltpu.VMEM((chunks,) + split[2:], bf16),
            pltpu.VMEM((chunks,) + split[2:], bf16),
            pltpu.VMEM((chunks, FAN - 1) + split[3:], bf16),
            pltpu.VMEM((chunks, FAN - 1) + split[3:], bf16),
            pltpu.VMEM((chunks, far_rounds) + split[3:], bf16),
            pltpu.VMEM((chunks, far_rounds) + split[3:], bf16),
            dma((2, 2, 2)),
            dma((2, chunks, 2)),
            dma((2, chunks, 2)),
            dma((2, chunks, FAN - 1, 2)),
            dma((chunks, far_rounds, 2)),
            dma((5,)),
        ],
        compiler_params=pltpu.CompilerParams(
            collective_id=0, has_side_effects=True, vmem_limit_bytes=60 * 2**20
        ),
        cost_estimate=pl.CostEstimate(flops=flops, bytes_accessed=2**23, transcendentals=0),
        name="tile_conv_step",
    )(features, weights, grad_out, tile_pos, neighbours)
    return pl.pallas_call(
        finish,
        out_shape=(
            jax.ShapeDtypeStruct(act.shape, bf16),
            jax.ShapeDtypeStruct(weights.shape, f32),
            jax.ShapeDtypeStruct(act.shape, bf16),
        ),
        in_specs=[vmem] * 3,
        out_specs=(hbm, hbm, hbm),
        scratch_shapes=[
            pltpu.VMEM(weights.shape, f32),
            dma((2 + chunks,)),
        ],
        compiler_params=pltpu.CompilerParams(vmem_limit_bytes=8 * 2**20),
        name="write_results",
    )(act, grad_sum, input_grad)


def solution(mesh):
    in_specs = (
        P(("groups", "tile"), None, None, None),
        P(),
        P(("groups", "tile"), None, None, None),
        P(("groups", "tile")),
        P(("groups", "tile"), None),
    )
    out_specs = (
        P(("groups", "tile"), None, None, None),
        P("groups", None, None),
        P(("groups", "tile"), None, None, None),
    )
    return jax.shard_map(
        functools.partial(body, mesh.shape["tile"]),
        mesh=mesh,
        in_specs=in_specs,
        out_specs=out_specs,
        check_vma=False,
    )
```

```python
import functools
import math

import jax
import jax.numpy as jnp
from jax import lax
from jax.experimental import pallas as pl
from jax.experimental.pallas import tpu as pltpu
from jax.sharding import PartitionSpec as P

ROOT_HALF = 0.7071067811865476
INV_ROOT_TAU = 0.3989422804014327
FAN = 4
GROUP = 3
CHUNK = 1
LAG_CORE, LAG_NEAR, LAG_FAN, LAG_FAN_BACK, LAG_NEAR_BACK, LAG_CORE_BACK = (1, 3, 5, 7, 9, 10)
MESH = pl.DeviceIdType.MESH


def shifted(center, left, right, axis):
    cell = lax.broadcasted_iota(jnp.int32, center.shape, axis)
    side = center.shape[axis]
    from_left = pltpu.roll(jnp.where(cell == side - 1, left, center), 1, axis)
    from_right = pltpu.roll(jnp.where(cell == 0, right, center), side - 1, axis)
    return from_left, from_right


def kernel(
    count,
    scale,
    features_hbm,
    weights_hbm,
    grad_out_hbm,
    tile_pos_hbm,
    links_hbm,
    act,
    total,
    input_grad,
    features,
    weights,
    grad_out,
    tile_pos,
    links,
    ext_x,
    ext_g,
    above_x,
    below_x,
    above_g,
    below_g,
    rows_out,
    pre_grad,
    pre_grad_t,
    weights_t,
    part,
    core_out,
    core_in,
    near_out,
    near_in,
    fan_out,
    fan_in,
    far_out,
    far_in,
    halo_sems,
    core_sems,
    near_sems,
    fan_sems,
    far_sems,
    load_sems,
):
    f32, bf16 = jnp.float32, jnp.bfloat16
    tiles, side, _, channels = features.shape
    cells = side * side
    taps = weights.shape[0]
    zero_row = 2 * tiles
    me = lax.axis_index("tile")
    core = lax.rem(me, 2)
    near = lax.rem(me // 2, 2)
    fan = lax.rem(me // 4, FAN)
    base = me - core - 2 * near - 4 * fan
    core_peer = me + 1 - 2 * core
    near_peer = me + 2 - 4 * near
    far_rounds = far_out.shape[1]

    def fan_slot(step):
        return lax.rem(fan + step + FAN, FAN)

    def fan_peer(step):
        return base + 4 * fan_slot(step) + 2 * near + core

    def far_peer(turn):
        stride = 4 * FAN * 2**turn
        return me + stride - 2 * stride * lax.rem(me // stride, 2)

    def send(source, target, sems, peer):
        return pltpu.make_async_remote_copy(
            src_ref=source,
            dst_ref=target,
            send_sem=sems.at[0],
            recv_sem=sems.at[1],
            device_id={"tile": peer},
            device_id_type=MESH,
        )

    pairs = (
        (features_hbm, features),
        (links_hbm, links),
        (weights_hbm, weights),
        (tile_pos_hbm, tile_pos),
        (grad_out_hbm, grad_out),
    )
    loads = [pltpu.make_async_copy(*pair, load_sems.at[at]) for at, pair in enumerate(pairs)]
    for load in loads:
        load.start()

    has_prev, has_next = me > 0, me < count - 1
    barrier = pltpu.get_barrier_semaphore()
    peers = [core_peer, near_peer] + [fan_peer(step) for step in range(1, FAN)]
    peers = peers + [far_peer(turn) for turn in range(far_rounds)]
    for peer in peers:
        pl.semaphore_signal(barrier, inc=1, device_id={"tile": peer}, device_id_type=MESH)

    @pl.when(has_prev)
    def _():
        pl.semaphore_signal(barrier, inc=1, device_id={"tile": me - 1}, device_id_type=MESH)

    @pl.when(has_next)
    def _():
        pl.semaphore_signal(barrier, inc=1, device_id={"tile": me + 1}, device_id_type=MESH)

    pl.semaphore_wait(barrier, len(peers) + jnp.where(has_prev, 1, 0) + jnp.where(has_next, 1, 0))

    def halo(turn, above, below):
        down = send(rows_out.at[turn, 0], above.at[pl.ds(0, tiles)], halo_sems.at[turn, 0], me + 1)
        up = send(rows_out.at[turn, 1], below.at[pl.ds(tiles, tiles)], halo_sems.at[turn, 1], me - 1)
        return down, up

    def start_halo(turn, field, above, below):
        last, first = field[:, side - 1], field[:, 0]
        rows_out[turn, 0] = last
        rows_out[turn, 1] = first
        down, up = halo(turn, above, below)

        @pl.when(has_next)
        def _():
            down.start()

        @pl.when(has_prev)
        def _():
            up.start()

        above[tiles : 2 * tiles] = last
        below[0:tiles] = first
        for table in (above, below):
            table[zero_row] = jnp.zeros(table.shape[1:], table.dtype)

    def wait_halo(turn, above, below):
        down, up = halo(turn, above, below)

        @pl.when(has_next)
        def _():
            down.wait_send()
            up.wait_recv()

        @pl.when(has_prev)
        def _():
            up.wait_send()
            down.wait_recv()

    def link_gate(code):
        return jnp.where(code >= 0, 1.0, 0.0).astype(f32)

    def inner_rows(field, tile, put):
        center = field[tile]
        left, right = links[tile, 2], links[tile, 3]
        left_map = field[jnp.where(left >= tiles, left - tiles, tile)].astype(f32) * link_gate(left)
        right_map = field[jnp.where(right >= tiles, right - tiles, tile)].astype(f32) * link_gate(right)
        from_left, from_right = shifted(center.astype(f32), left_map, right_map, 1)
        inner = slice(1, side + 1)
        put(0, inner, from_left.astype(bf16))
        put(1, inner, center)
        put(2, inner, from_right.astype(bf16))

    def border_rows(table, row, tile, first_link, left_link, right_link, base_code, put):
        def pick(link):
            code = links[tile, link]
            return table[jnp.where(code >= base_code, code - base_code, zero_row)]

        center = pick(first_link)
        from_left, from_right = shifted(
            center.astype(f32), pick(left_link).astype(f32), pick(right_link).astype(f32), 0
        )
        put(0, row, from_left.astype(bf16))
        put(1, row, center)
        put(2, row, from_right.astype(bf16))

    def both_borders(above, below, tile, put):
        border_rows(above, 0, tile, 0, 4, 5, 0, put)
        border_rows(below, side + 1, tile, 1, 6, 7, tiles, put)

    loads[0].wait()
    loads[1].wait()

    start_halo(0, features, above_x, below_x)

    def put_x(tile):
        def put(shift, rows, value):
            ext_x[shift, tile, rows] = value

        return put

    @pl.loop(0, tiles)
    def _(tile):
        inner_rows(features, tile, put_x(tile))

    wait_halo(0, above_x, below_x)

    for tile in range(tiles):
        both_borders(above_x, below_x, tile, put_x(tile))

    for load in loads[2:]:
        load.wait()

    weight_mat_rows = taps * channels

    def forward_dot(tile):
        pieces = [
            ext_x[b, tile, a : a + side].reshape(cells, channels) for a in range(3) for b in range(3)
        ]
        return jnp.dot(
            jnp.concatenate(pieces, axis=1),
            weights[...].reshape(weight_mat_rows, channels),
            preferred_element_type=f32,
        )

    def forward_point(tile, preact):
        gate = jnp.where(tile_pos[tile] >= 0, 1.0, 0.0).astype(f32)
        cumulative = 0.5 * (1.0 + lax.erf(preact * ROOT_HALF))
        density = jnp.exp(-0.5 * preact * preact) * INV_ROOT_TAU
        act[tile] = (preact * cumulative * gate).astype(bf16).reshape(side, side, channels)
        grad = grad_out[tile].reshape(cells, channels).astype(f32)
        slope = grad * (cumulative + preact * density) * gate
        pre_grad[tile] = slope.astype(bf16).reshape(side, side, channels)
        pre_grad_t[tile] = slope.T.astype(bf16)

    batch = GROUP if tiles % GROUP == 0 else 1

    @pl.loop(0, tiles // batch)
    def _(turn):
        group = [turn * batch + at for at in range(batch)]
        preacts = [forward_dot(tile) for tile in group]
        for tile, preact in zip(group, preacts):
            forward_point(tile, preact)

    start_halo(1, pre_grad, above_g, below_g)

    def core_copy(k):
        return send(core_out.at[k], core_in.at[k], core_sems.at[0, k], core_peer)

    def near_copy(k):
        return send(near_out.at[k], near_in.at[k], near_sems.at[0, k], near_peer)

    def fan_copy(k, step):
        return send(
            fan_out.at[k, step - 1],
            fan_in.at[k, step - 1],
            fan_sems.at[0, k, step - 1],
            fan_peer(step),
        )

    def far_copy(k, turn):
        return send(far_out.at[k, turn], far_in.at[k, turn], far_sems.at[k, turn], far_peer(turn))

    def fan_back(k, step, owner):
        block = total.at[k, core, near, owner]
        return send(block, block, fan_sems.at[1, k, step - 1], fan_peer(step))

    def near_back(k, owner):
        block = total.at[k, core, owner]
        return send(block, block, near_sems.at[1, k], near_peer)

    def core_back(k, owner):
        block = total.at[k, owner]
        return send(block, block, core_sems.at[1, k], core_peer)

    def put_g(tile):
        def put(shift, rows, value):
            ext_g[shift, tile, rows] = value

        return put

    chunks = part.shape[0]
    width = taps // chunks

    def due(step, lag):
        since = step - lag - (width - 1)
        return (since >= 0) & (since < taps) & (lax.rem(since, width) == 0)

    def chunk_of(step, lag):
        return (step - lag - (width - 1)) // width

    @pl.loop(0, taps + LAG_CORE_BACK)
    def _(step):
        @pl.when(step < taps)
        def _():
            k = step
            rows = ext_x[lax.rem(k, 3), :, pl.ds(k // 3, side)].reshape(tiles * cells, channels)
            lhs = jnp.concatenate([pre_grad_t[tile] for tile in range(tiles)], axis=1)
            term = jnp.dot(lhs, rows, preferred_element_type=f32)
            chunk, at = k // width, lax.rem(k, width)
            part[chunk, :, :, :, at] = term.T.reshape(part.shape[1:4] + part.shape[5:])
            core_out[chunk, :, :, at] = part[chunk, 1 - core, :, :, at].astype(bf16)

            @pl.when(at == width - 1)
            def _():
                core_copy(chunk).start()


        @pl.when(due(step, LAG_CORE))
        def _():
            k = chunk_of(step, LAG_CORE)
            core_copy(k).wait_recv()
            part[k, core] = part[k, core] + core_in[k].astype(f32)
            near_out[k] = part[k, core, 1 - near].astype(bf16)
            near_copy(k).start()

        @pl.when(due(step, LAG_NEAR))
        def _():
            k = chunk_of(step, LAG_NEAR)
            near_copy(k).wait_recv()
            part[k, core, near] = part[k, core, near] + near_in[k].astype(f32)
            for turn in range(1, FAN):
                fan_out[k, turn - 1] = part[k, core, near, fan_slot(turn)].astype(bf16)
                fan_copy(k, turn).start()

        @pl.when(due(step, LAG_FAN))
        def _():
            k = chunk_of(step, LAG_FAN)
            sums = part[k, core, near, fan]
            for turn in range(1, FAN):
                fan_copy(k, turn).wait_recv()
                sums = sums + fan_in[k, turn - 1].astype(f32)
            for turn in range(far_rounds):
                far_out[k, turn] = sums.astype(bf16)
                copy = far_copy(k, turn)
                copy.start()
                copy.wait()
                sums = far_out[k, turn].astype(f32) + far_in[k, turn].astype(f32)
            total[k, core, near, fan] = (sums * scale).astype(bf16)
            for turn in range(1, FAN):
                fan_back(k, turn, fan).start()

        @pl.when(due(step, LAG_FAN_BACK))
        def _():
            k = chunk_of(step, LAG_FAN_BACK)
            for turn in range(1, FAN):
                fan_back(k, turn, fan_slot(-turn)).wait_recv()
            near_back(k, near).start()

        @pl.when(due(step, LAG_NEAR_BACK))
        def _():
            k = chunk_of(step, LAG_NEAR_BACK)
            near_back(k, 1 - near).wait_recv()
            core_back(k, core).start()

        @pl.when(due(step, LAG_CORE_BACK))
        def _():
            k = chunk_of(step, LAG_CORE_BACK)
            core_back(k, 1 - core).wait_recv()
            core_copy(k).wait_send()
            near_copy(k).wait_send()
            for turn in range(1, FAN):
                fan_copy(k, turn).wait_send()
                fan_back(k, turn, fan).wait_send()
            near_back(k, near).wait_send()
            core_back(k, core).wait_send()

        @pl.when(step == taps)
        def _():
            wait_halo(1, above_g, below_g)
            for tile in range(tiles):
                both_borders(above_g, below_g, tile, put_g(tile))

        @pl.when((step >= taps) & (step < taps + 3))
        def _():
            for at in range(taps // 3):
                tap = (step - taps) * (taps // 3) + at
                weights_t[tap] = weights[tap].astype(f32).T.astype(bf16)
            for at in range(tiles // 3):
                tile = (step - taps) * (tiles // 3) + at
                inner_rows(pre_grad, tile, put_g(tile))

        @pl.when((step >= taps + 3) & (step < taps + 3 + tiles))
        def _():
            tile = step - taps - 3
            pieces = [
                ext_g[2 - b, tile, 2 - a : 2 - a + side].reshape(cells, channels)
                for a in range(3)
                for b in range(3)
            ]
            back = jnp.dot(
                jnp.concatenate(pieces, axis=1),
                weights_t[...].reshape(weight_mat_rows, channels),
                preferred_element_type=f32,
            )
            gate = jnp.where(tile_pos[tile] >= 0, 1.0, 0.0).astype(f32)
            input_grad[tile] = (back * gate).astype(bf16).reshape(side, side, channels)


def finish(act_in, grad_in, back_in, act_out, grad_out, back_out, wide, sems):
    taps = wide.shape[0]
    copies = [
        pltpu.make_async_copy(back_in, back_out, sems.at[0]),
        pltpu.make_async_copy(act_in, act_out, sems.at[1]),
    ]
    for copy in copies:
        copy.start()
    chunks, width = grad_in.shape[0], grad_in.shape[4]
    for chunk in range(chunks):
        for at in range(width):
            block = grad_in[chunk, :, :, :, at].astype(jnp.float32)
            wide[chunk * width + at] = block.reshape(wide.shape[1:])
        rows = pl.ds(chunk * width, width)
        copies.append(pltpu.make_async_copy(wide.at[rows], grad_out.at[rows], sems.at[len(copies)]))
        copies[-1].start()
    for copy in copies:
        copy.wait()


def body(count, features, weights, grad_out, tile_pos, neighbours):
    bf16, f32 = jnp.bfloat16, jnp.float32
    tiles, side, _, channels = features.shape
    taps = weights.shape[0]
    scale = 1.0 / math.sqrt(tiles * count * side * side)
    chunks = taps // CHUNK
    split = (2, 2, FAN, CHUNK, channels // (4 * FAN), channels)
    far_rounds = int(math.log2(count // (4 * FAN)))
    table = pltpu.VMEM((2 * tiles + 1, side, channels), bf16)
    dma = pltpu.SemaphoreType.DMA
    hbm = pl.BlockSpec(memory_space=pl.ANY)
    vmem = pl.BlockSpec(memory_space=pltpu.VMEM)
    flops = 3 * 2 * tiles * side * side * taps * channels * channels
    act, grad_sum, input_grad = pl.pallas_call(
        functools.partial(kernel, count, scale),
        out_shape=(
            pltpu.VMEM(features.shape, bf16),
            pltpu.VMEM((chunks,) + split, bf16),
            pltpu.VMEM(features.shape, bf16),
        ),
        in_specs=[hbm] * 5,
        out_specs=(vmem, vmem, vmem),
        scratch_shapes=[
            pltpu.VMEM(features.shape, bf16),
            pltpu.VMEM(weights.shape, bf16),
            pltpu.VMEM(features.shape, bf16),
            pltpu.SMEM(tile_pos.shape, jnp.int32),
            pltpu.SMEM(neighbours.shape, jnp.int32),
            pltpu.VMEM((3, tiles, side + 2, side, channels), bf16),
            pltpu.VMEM((3, tiles, side + 2, side, channels), bf16),
            table,
            table,
            table,
            table,
            pltpu.VMEM((2, 2, tiles, side, channels), bf16),
            pltpu.VMEM(features.shape, bf16),
            pltpu.VMEM((tiles, channels, side * side), bf16),
            pltpu.VMEM(weights.shape, bf16),
            pltpu.VMEM((chunks,) + split, f32),
            pltpu.VMEM((chunks,) + split[1:], bf16),
            pltpu.VMEM((chunks,) + split[1:], bf16),
            pltpu.VMEM((chunks,) + split[2:], bf16),
            pltpu.VMEM((chunks,) + split[2:], bf16),
            pltpu.VMEM((chunks, FAN - 1) + split[3:], bf16),
            pltpu.VMEM((chunks, FAN - 1) + split[3:], bf16),
            pltpu.VMEM((chunks, far_rounds) + split[3:], bf16),
            pltpu.VMEM((chunks, far_rounds) + split[3:], bf16),
            dma((2, 2, 2)),
            dma((2, chunks, 2)),
            dma((2, chunks, 2)),
            dma((2, chunks, FAN - 1, 2)),
            dma((chunks, far_rounds, 2)),
            dma((5,)),
        ],
        compiler_params=pltpu.CompilerParams(
            collective_id=0, has_side_effects=True, vmem_limit_bytes=60 * 2**20
        ),
        cost_estimate=pl.CostEstimate(flops=flops, bytes_accessed=2**23, transcendentals=0),
        name="tile_conv_step",
    )(features, weights, grad_out, tile_pos, neighbours)
    return pl.pallas_call(
        finish,
        out_shape=(
            jax.ShapeDtypeStruct(act.shape, bf16),
            jax.ShapeDtypeStruct(weights.shape, f32),
            jax.ShapeDtypeStruct(act.shape, bf16),
        ),
        in_specs=[vmem] * 3,
        out_specs=(hbm, hbm, hbm),
        scratch_shapes=[
            pltpu.VMEM(weights.shape, f32),
            dma((2 + chunks,)),
        ],
        compiler_params=pltpu.CompilerParams(vmem_limit_bytes=8 * 2**20),
        name="write_results",
    )(act, grad_sum, input_grad)


def solution(mesh):
    in_specs = (
        P(("groups", "tile"), None, None, None),
        P(),
        P(("groups", "tile"), None, None, None),
        P(("groups", "tile")),
        P(("groups", "tile"), None),
    )
    out_specs = (
        P(("groups", "tile"), None, None, None),
        P("groups", None, None),
        P(("groups", "tile"), None, None, None),
    )
    return jax.shard_map(
        functools.partial(body, mesh.shape["tile"]),
        mesh=mesh,
        in_specs=in_specs,
        out_specs=out_specs,
        check_vma=False,
    )
```

```python
import functools
import math

import jax
import jax.numpy as jnp
from jax import lax
from jax.experimental import pallas as pl
from jax.experimental.pallas import tpu as pltpu
from jax.sharding import PartitionSpec as P

ROOT_HALF = 0.7071067811865476
INV_ROOT_TAU = 0.3989422804014327
HALVINGS = 4
GROUP = 3
CHUNK = 1
SEND_LAGS = (1, 3, 5, 7)
BACK_LAGS = (14, 13, 11, 9)
MESH = pl.DeviceIdType.MESH


def shifted(center, left, right, axis):
    cell = lax.broadcasted_iota(jnp.int32, center.shape, axis)
    side = center.shape[axis]
    from_left = pltpu.roll(jnp.where(cell == side - 1, left, center), 1, axis)
    from_right = pltpu.roll(jnp.where(cell == 0, right, center), side - 1, axis)
    return from_left, from_right


def kernel(
    count,
    scale,
    features_hbm,
    weights_hbm,
    grad_out_hbm,
    tile_pos_hbm,
    links_hbm,
    act,
    total,
    input_grad,
    features,
    weights,
    grad_out,
    tile_pos,
    links,
    ext_x,
    ext_g,
    above_x,
    below_x,
    above_g,
    below_g,
    rows_out,
    pre_grad,
    pre_grad_t,
    weights_t,
    part,
    outs,
    ins,
    far_out,
    far_in,
    halo_sems,
    out_sems,
    back_sems,
    far_sems,
    load_sems,
):
    f32, bf16 = jnp.float32, jnp.bfloat16
    tiles, side, _, channels = features.shape
    cells = side * side
    taps = weights.shape[0]
    zero_row = 2 * tiles
    me = lax.axis_index("tile")
    bits = [lax.rem(me // 2**at, 2) for at in range(HALVINGS)]
    peers = [me + 2**at * (1 - 2 * bits[at]) for at in range(HALVINGS)]
    far_rounds = far_out.shape[1]

    def far_peer(turn):
        stride = 2 ** (HALVINGS + turn)
        return me + stride - 2 * stride * lax.rem(me // stride, 2)

    def send(source, target, sems, peer):
        return pltpu.make_async_remote_copy(
            src_ref=source,
            dst_ref=target,
            send_sem=sems.at[0],
            recv_sem=sems.at[1],
            device_id={"tile": peer},
            device_id_type=MESH,
        )

    pairs = (
        (features_hbm, features),
        (links_hbm, links),
        (weights_hbm, weights),
        (tile_pos_hbm, tile_pos),
        (grad_out_hbm, grad_out),
    )
    loads = [pltpu.make_async_copy(*pair, load_sems.at[at]) for at, pair in enumerate(pairs)]
    for load in loads:
        load.start()

    has_prev, has_next = me > 0, me < count - 1
    barrier = pltpu.get_barrier_semaphore()
    greeted = peers + [far_peer(turn) for turn in range(far_rounds)]
    for peer in greeted:
        pl.semaphore_signal(barrier, inc=1, device_id={"tile": peer}, device_id_type=MESH)

    @pl.when(has_prev)
    def _():
        pl.semaphore_signal(barrier, inc=1, device_id={"tile": me - 1}, device_id_type=MESH)

    @pl.when(has_next)
    def _():
        pl.semaphore_signal(barrier, inc=1, device_id={"tile": me + 1}, device_id_type=MESH)

    pl.semaphore_wait(barrier, len(greeted) + jnp.where(has_prev, 1, 0) + jnp.where(has_next, 1, 0))

    def halo(turn, above, below):
        down = send(rows_out.at[turn, 0], above.at[pl.ds(0, tiles)], halo_sems.at[turn, 0], me + 1)
        up = send(rows_out.at[turn, 1], below.at[pl.ds(tiles, tiles)], halo_sems.at[turn, 1], me - 1)
        return down, up

    def start_halo(turn, field, above, below):
        last, first = field[:, side - 1], field[:, 0]
        rows_out[turn, 0] = last
        rows_out[turn, 1] = first
        down, up = halo(turn, above, below)

        @pl.when(has_next)
        def _():
            down.start()

        @pl.when(has_prev)
        def _():
            up.start()

        above[tiles : 2 * tiles] = last
        below[0:tiles] = first
        for table in (above, below):
            table[zero_row] = jnp.zeros(table.shape[1:], table.dtype)

    def wait_halo(turn, above, below):
        down, up = halo(turn, above, below)

        @pl.when(has_next)
        def _():
            down.wait_send()
            up.wait_recv()

        @pl.when(has_prev)
        def _():
            up.wait_send()
            down.wait_recv()

    def link_gate(code):
        return jnp.where(code >= 0, 1.0, 0.0).astype(f32)

    def inner_rows(field, tile, put):
        center = field[tile]
        left, right = links[tile, 2], links[tile, 3]
        left_map = field[jnp.where(left >= tiles, left - tiles, tile)].astype(f32) * link_gate(left)
        right_map = field[jnp.where(right >= tiles, right - tiles, tile)].astype(f32) * link_gate(right)
        from_left, from_right = shifted(center.astype(f32), left_map, right_map, 1)
        inner = slice(1, side + 1)
        put(0, inner, from_left.astype(bf16))
        put(1, inner, center)
        put(2, inner, from_right.astype(bf16))

    def border_rows(table, row, tile, first_link, left_link, right_link, base_code, put):
        def pick(link):
            code = links[tile, link]
            return table[jnp.where(code >= base_code, code - base_code, zero_row)]

        center = pick(first_link)
        from_left, from_right = shifted(
            center.astype(f32), pick(left_link).astype(f32), pick(right_link).astype(f32), 0
        )
        put(0, row, from_left.astype(bf16))
        put(1, row, center)
        put(2, row, from_right.astype(bf16))

    def both_borders(above, below, tile, put):
        border_rows(above, 0, tile, 0, 4, 5, 0, put)
        border_rows(below, side + 1, tile, 1, 6, 7, tiles, put)

    loads[0].wait()
    loads[1].wait()

    start_halo(0, features, above_x, below_x)

    def put_x(tile):
        def put(shift, rows, value):
            ext_x[shift, tile, rows] = value

        return put

    @pl.loop(0, tiles)
    def _(tile):
        inner_rows(features, tile, put_x(tile))

    wait_halo(0, above_x, below_x)

    for tile in range(tiles):
        both_borders(above_x, below_x, tile, put_x(tile))

    for load in loads[2:]:
        load.wait()

    weight_mat_rows = taps * channels

    def forward_dot(tile):
        pieces = [
            ext_x[b, tile, a : a + side].reshape(cells, channels) for a in range(3) for b in range(3)
        ]
        return jnp.dot(
            jnp.concatenate(pieces, axis=1),
            weights[...].reshape(weight_mat_rows, channels),
            preferred_element_type=f32,
        )

    def forward_point(tile, preact):
        gate = jnp.where(tile_pos[tile] >= 0, 1.0, 0.0).astype(f32)
        cumulative = 0.5 * (1.0 + lax.erf(preact * ROOT_HALF))
        density = jnp.exp(-0.5 * preact * preact) * INV_ROOT_TAU
        act[tile] = (preact * cumulative * gate).astype(bf16).reshape(side, side, channels)
        grad = grad_out[tile].reshape(cells, channels).astype(f32)
        slope = grad * (cumulative + preact * density) * gate
        pre_grad[tile] = slope.astype(bf16).reshape(side, side, channels)
        pre_grad_t[tile] = slope.T.astype(bf16)

    batch = GROUP if tiles % GROUP == 0 else 1

    @pl.loop(0, tiles // batch)
    def _(turn):
        group = [turn * batch + at for at in range(batch)]
        preacts = [forward_dot(tile) for tile in group]
        for tile, preact in zip(group, preacts):
            forward_point(tile, preact)

    start_halo(1, pre_grad, above_g, below_g)

    def out_copy(at, k):
        return send(outs[at].at[k], ins[at].at[k], out_sems.at[at, k], peers[at])

    def back_copy(at, k, owner):
        block = total.at[(k, *bits[:at], owner)]
        return send(block, block, back_sems.at[at, k], peers[at])

    def far_copy(k, turn):
        return send(far_out.at[k, turn], far_in.at[k, turn], far_sems.at[k, turn], far_peer(turn))

    def put_g(tile):
        def put(shift, rows, value):
            ext_g[shift, tile, rows] = value

        return put

    chunks = part.shape[0]
    width = taps // chunks

    def due(step, lag):
        since = step - lag - (width - 1)
        return (since >= 0) & (since < taps) & (lax.rem(since, width) == 0)

    def chunk_of(step, lag):
        return (step - lag - (width - 1)) // width

    @pl.loop(0, taps + BACK_LAGS[0])
    def _(step):
        @pl.when(step < taps)
        def _():
            k = step
            rows = ext_x[lax.rem(k, 3), :, pl.ds(k // 3, side)].reshape(tiles * cells, channels)
            lhs = jnp.concatenate([pre_grad_t[tile] for tile in range(tiles)], axis=1)
            term = jnp.dot(lhs, rows, preferred_element_type=f32)
            chunk, at = k // width, lax.rem(k, width)
            part[chunk, :, :, :, :, at] = term.T.reshape(part.shape[1:5] + part.shape[6:])
            outs[0][chunk, :, :, :, at] = part[chunk, 1 - bits[0], :, :, :, at].astype(bf16)

            @pl.when(at == width - 1)
            def _():
                out_copy(0, chunk).start()


        for at in range(HALVINGS - 1):

            @pl.when(due(step, SEND_LAGS[at]))
            def _(at=at):
                k = chunk_of(step, SEND_LAGS[at])
                out_copy(at, k).wait_recv()
                mine = (k, *bits[: at + 1])
                part[mine] = part[mine] + ins[at][k].astype(f32)
                outs[at + 1][k] = part[(*mine, 1 - bits[at + 1])].astype(bf16)
                out_copy(at + 1, k).start()

        @pl.when(due(step, SEND_LAGS[-1]))
        def _():
            k = chunk_of(step, SEND_LAGS[-1])
            out_copy(HALVINGS - 1, k).wait_recv()
            sums = part[(k, *bits)] + ins[HALVINGS - 1][k].astype(f32)
            for turn in range(far_rounds):
                far_out[k, turn] = sums.astype(bf16)
                copy = far_copy(k, turn)
                copy.start()
                copy.wait()
                sums = far_out[k, turn].astype(f32) + far_in[k, turn].astype(f32)
            total[(k, *bits)] = (sums * scale).astype(bf16)
            back_copy(HALVINGS - 1, k, bits[-1]).start()

        for at in range(HALVINGS - 1, 0, -1):

            @pl.when(due(step, BACK_LAGS[at]))
            def _(at=at):
                k = chunk_of(step, BACK_LAGS[at])
                back_copy(at, k, 1 - bits[at]).wait_recv()
                back_copy(at - 1, k, bits[at - 1]).start()

        @pl.when(due(step, BACK_LAGS[0]))
        def _():
            k = chunk_of(step, BACK_LAGS[0])
            back_copy(0, k, 1 - bits[0]).wait_recv()
            for at in range(HALVINGS):
                out_copy(at, k).wait_send()
                back_copy(at, k, bits[at]).wait_send()

        @pl.when(step == taps)
        def _():
            wait_halo(1, above_g, below_g)
            for tile in range(tiles):
                both_borders(above_g, below_g, tile, put_g(tile))

        @pl.when((step >= taps) & (step < taps + 3))
        def _():
            for at in range(taps // 3):
                tap = (step - taps) * (taps // 3) + at
                weights_t[tap] = weights[tap].astype(f32).T.astype(bf16)
            for at in range(tiles // 3):
                tile = (step - taps) * (tiles // 3) + at
                inner_rows(pre_grad, tile, put_g(tile))

        @pl.when((step >= taps + 3) & (step < taps + 3 + tiles))
        def _():
            tile = step - taps - 3
            pieces = [
                ext_g[2 - b, tile, 2 - a : 2 - a + side].reshape(cells, channels)
                for a in range(3)
                for b in range(3)
            ]
            back = jnp.dot(
                jnp.concatenate(pieces, axis=1),
                weights_t[...].reshape(weight_mat_rows, channels),
                preferred_element_type=f32,
            )
            gate = jnp.where(tile_pos[tile] >= 0, 1.0, 0.0).astype(f32)
            input_grad[tile] = (back * gate).astype(bf16).reshape(side, side, channels)


def finish(act_in, grad_in, back_in, act_out, grad_out, back_out, wide, sems):
    taps = wide.shape[0]
    copies = [
        pltpu.make_async_copy(back_in, back_out, sems.at[0]),
        pltpu.make_async_copy(act_in, act_out, sems.at[1]),
    ]
    for copy in copies:
        copy.start()
    chunks, width = grad_in.shape[0], grad_in.shape[HALVINGS + 1]
    for chunk in range(chunks):
        for at in range(width):
            block = grad_in[chunk, :, :, :, :, at].astype(jnp.float32)
            wide[chunk * width + at] = block.reshape(wide.shape[1:])
        rows = pl.ds(chunk * width, width)
        copies.append(pltpu.make_async_copy(wide.at[rows], grad_out.at[rows], sems.at[len(copies)]))
        copies[-1].start()
    for copy in copies:
        copy.wait()


def body(count, features, weights, grad_out, tile_pos, neighbours):
    bf16, f32 = jnp.bfloat16, jnp.float32
    tiles, side, _, channels = features.shape
    taps = weights.shape[0]
    scale = 1.0 / math.sqrt(tiles * count * side * side)
    chunks = taps // CHUNK
    split = (2,) * HALVINGS + (CHUNK, channels // 2**HALVINGS, channels)
    far_rounds = int(math.log2(count // 2**HALVINGS))
    table = pltpu.VMEM((2 * tiles + 1, side, channels), bf16)
    dma = pltpu.SemaphoreType.DMA
    hbm = pl.BlockSpec(memory_space=pl.ANY)
    vmem = pl.BlockSpec(memory_space=pltpu.VMEM)
    halves = [pltpu.VMEM((chunks,) + split[at + 1 :], bf16) for at in range(HALVINGS)]
    flops = 3 * 2 * tiles * side * side * taps * channels * channels
    act, grad_sum, input_grad = pl.pallas_call(
        functools.partial(kernel, count, scale),
        out_shape=(
            pltpu.VMEM(features.shape, bf16),
            pltpu.VMEM((chunks,) + split, bf16),
            pltpu.VMEM(features.shape, bf16),
        ),
        in_specs=[hbm] * 5,
        out_specs=(vmem, vmem, vmem),
        scratch_shapes=[
            pltpu.VMEM(features.shape, bf16),
            pltpu.VMEM(weights.shape, bf16),
            pltpu.VMEM(features.shape, bf16),
            pltpu.SMEM(tile_pos.shape, jnp.int32),
            pltpu.SMEM(neighbours.shape, jnp.int32),
            pltpu.VMEM((3, tiles, side + 2, side, channels), bf16),
            pltpu.VMEM((3, tiles, side + 2, side, channels), bf16),
            table,
            table,
            table,
            table,
            pltpu.VMEM((2, 2, tiles, side, channels), bf16),
            pltpu.VMEM(features.shape, bf16),
            pltpu.VMEM((tiles, channels, side * side), bf16),
            pltpu.VMEM(weights.shape, bf16),
            pltpu.VMEM((chunks,) + split, f32),
            halves,
            halves,
            pltpu.VMEM((chunks, far_rounds) + split[HALVINGS:], bf16),
            pltpu.VMEM((chunks, far_rounds) + split[HALVINGS:], bf16),
            dma((2, 2, 2)),
            dma((HALVINGS, chunks, 2)),
            dma((HALVINGS, chunks, 2)),
            dma((chunks, far_rounds, 2)),
            dma((5,)),
        ],
        compiler_params=pltpu.CompilerParams(
            collective_id=0, has_side_effects=True, vmem_limit_bytes=60 * 2**20
        ),
        cost_estimate=pl.CostEstimate(flops=flops, bytes_accessed=2**23, transcendentals=0),
        name="tile_conv_step",
    )(features, weights, grad_out, tile_pos, neighbours)
    return pl.pallas_call(
        finish,
        out_shape=(
            jax.ShapeDtypeStruct(act.shape, bf16),
            jax.ShapeDtypeStruct(weights.shape, f32),
            jax.ShapeDtypeStruct(act.shape, bf16),
        ),
        in_specs=[vmem] * 3,
        out_specs=(hbm, hbm, hbm),
        scratch_shapes=[
            pltpu.VMEM(weights.shape, f32),
            dma((2 + chunks,)),
        ],
        compiler_params=pltpu.CompilerParams(vmem_limit_bytes=8 * 2**20),
        name="write_results",
    )(act, grad_sum, input_grad)


def solution(mesh):
    in_specs = (
        P(("groups", "tile"), None, None, None),
        P(),
        P(("groups", "tile"), None, None, None),
        P(("groups", "tile")),
        P(("groups", "tile"), None),
    )
    out_specs = (
        P(("groups", "tile"), None, None, None),
        P("groups", None, None),
        P(("groups", "tile"), None, None, None),
    )
    return jax.shard_map(
        functools.partial(body, mesh.shape["tile"]),
        mesh=mesh,
        in_specs=in_specs,
        out_specs=out_specs,
        check_vma=False,
    )
```

```python
import functools
import math

import jax
import jax.numpy as jnp
from jax import lax
from jax.experimental import pallas as pl
from jax.experimental.pallas import tpu as pltpu
from jax.sharding import PartitionSpec as P

ROOT_HALF = 0.7071067811865476
INV_ROOT_TAU = 0.3989422804014327
FAN = 4
GROUP = 3
CHUNK = 1
LAG_CORE, LAG_NEAR, LAG_FAN, LAG_FAN_BACK, LAG_NEAR_BACK, LAG_CORE_BACK = (2, 5, 8, 11, 14, 16)
MESH = pl.DeviceIdType.MESH


def shifted(center, left, right, axis):
    cell = lax.broadcasted_iota(jnp.int32, center.shape, axis)
    side = center.shape[axis]
    from_left = pltpu.roll(jnp.where(cell == side - 1, left, center), 1, axis)
    from_right = pltpu.roll(jnp.where(cell == 0, right, center), side - 1, axis)
    return from_left, from_right


def kernel(
    count,
    scale,
    features_hbm,
    weights_hbm,
    grad_out_hbm,
    tile_pos_hbm,
    links_hbm,
    act,
    total,
    input_grad,
    features,
    weights,
    grad_out,
    tile_pos,
    links,
    ext_x,
    ext_g,
    above_x,
    below_x,
    above_g,
    below_g,
    rows_out,
    pre_grad,
    pre_grad_t,
    weights_t,
    part,
    core_out,
    core_in,
    near_out,
    near_in,
    fan_out,
    fan_in,
    far_out,
    far_in,
    halo_sems,
    core_sems,
    near_sems,
    fan_sems,
    far_sems,
    load_sems,
):
    f32, bf16 = jnp.float32, jnp.bfloat16
    tiles, side, _, channels = features.shape
    cells = side * side
    taps = weights.shape[0]
    zero_row = 2 * tiles
    me = lax.axis_index("tile")
    core = lax.rem(me, 2)
    near = lax.rem(me // 2, 2)
    fan = lax.rem(me // 4, FAN)
    base = me - core - 2 * near - 4 * fan
    core_peer = me + 1 - 2 * core
    near_peer = me + 2 - 4 * near
    far_rounds = far_out.shape[1]

    def fan_slot(step):
        return lax.rem(fan + step + FAN, FAN)

    def fan_peer(step):
        return base + 4 * fan_slot(step) + 2 * near + core

    def far_peer(turn):
        stride = 4 * FAN * 2**turn
        return me + stride - 2 * stride * lax.rem(me // stride, 2)

    def send(source, target, sems, peer):
        return pltpu.make_async_remote_copy(
            src_ref=source,
            dst_ref=target,
            send_sem=sems.at[0],
            recv_sem=sems.at[1],
            device_id={"tile": peer},
            device_id_type=MESH,
        )

    pairs = (
        (features_hbm, features),
        (links_hbm, links),
        (weights_hbm, weights),
        (tile_pos_hbm, tile_pos),
        (grad_out_hbm, grad_out),
    )
    loads = [pltpu.make_async_copy(*pair, load_sems.at[at]) for at, pair in enumerate(pairs)]
    for load in loads:
        load.start()

    has_prev, has_next = me > 0, me < count - 1
    barrier = pltpu.get_barrier_semaphore()
    peers = [core_peer, near_peer] + [fan_peer(step) for step in range(1, FAN)]
    peers = peers + [far_peer(turn) for turn in range(far_rounds)]
    for peer in peers:
        pl.semaphore_signal(barrier, inc=1, device_id={"tile": peer}, device_id_type=MESH)

    @pl.when(has_prev)
    def _():
        pl.semaphore_signal(barrier, inc=1, device_id={"tile": me - 1}, device_id_type=MESH)

    @pl.when(has_next)
    def _():
        pl.semaphore_signal(barrier, inc=1, device_id={"tile": me + 1}, device_id_type=MESH)

    pl.semaphore_wait(barrier, len(peers) + jnp.where(has_prev, 1, 0) + jnp.where(has_next, 1, 0))

    def halo(turn, above, below):
        down = send(rows_out.at[turn, 0], above.at[pl.ds(0, tiles)], halo_sems.at[turn, 0], me + 1)
        up = send(rows_out.at[turn, 1], below.at[pl.ds(tiles, tiles)], halo_sems.at[turn, 1], me - 1)
        return down, up

    def start_halo(turn, field, above, below):
        last, first = field[:, side - 1], field[:, 0]
        rows_out[turn, 0] = last
        rows_out[turn, 1] = first
        down, up = halo(turn, above, below)

        @pl.when(has_next)
        def _():
            down.start()

        @pl.when(has_prev)
        def _():
            up.start()

        above[tiles : 2 * tiles] = last
        below[0:tiles] = first
        for table in (above, below):
            table[zero_row] = jnp.zeros(table.shape[1:], table.dtype)

    def wait_halo(turn, above, below):
        down, up = halo(turn, above, below)

        @pl.when(has_next)
        def _():
            down.wait_send()
            up.wait_recv()

        @pl.when(has_prev)
        def _():
            up.wait_send()
            down.wait_recv()

    def link_gate(code):
        return jnp.where(code >= 0, 1.0, 0.0).astype(f32)

    def inner_rows(field, tile, put):
        center = field[tile]
        left, right = links[tile, 2], links[tile, 3]
        left_map = field[jnp.where(left >= tiles, left - tiles, tile)].astype(f32) * link_gate(left)
        right_map = field[jnp.where(right >= tiles, right - tiles, tile)].astype(f32) * link_gate(right)
        from_left, from_right = shifted(center.astype(f32), left_map, right_map, 1)
        inner = slice(1, side + 1)
        put(0, inner, from_left.astype(bf16))
        put(1, inner, center)
        put(2, inner, from_right.astype(bf16))

    def border_rows(table, row, tile, first_link, left_link, right_link, base_code, put):
        def pick(link):
            code = links[tile, link]
            return table[jnp.where(code >= base_code, code - base_code, zero_row)]

        center = pick(first_link)
        from_left, from_right = shifted(
            center.astype(f32), pick(left_link).astype(f32), pick(right_link).astype(f32), 0
        )
        put(0, row, from_left.astype(bf16))
        put(1, row, center)
        put(2, row, from_right.astype(bf16))

    def both_borders(above, below, tile, put):
        border_rows(above, 0, tile, 0, 4, 5, 0, put)
        border_rows(below, side + 1, tile, 1, 6, 7, tiles, put)

    loads[0].wait()
    loads[1].wait()

    start_halo(0, features, above_x, below_x)

    def put_x(tile):
        def put(shift, rows, value):
            ext_x[shift, tile, rows] = value

        return put

    @pl.loop(0, tiles)
    def _(tile):
        inner_rows(features, tile, put_x(tile))

    wait_halo(0, above_x, below_x)

    for tile in range(tiles):
        both_borders(above_x, below_x, tile, put_x(tile))

    for load in loads[2:]:
        load.wait()

    weight_mat_rows = taps * channels

    def forward_dot(tile):
        pieces = [
            ext_x[b, tile, a : a + side].reshape(cells, channels) for a in range(3) for b in range(3)
        ]
        return jnp.dot(
            jnp.concatenate(pieces, axis=1),
            weights[...].reshape(weight_mat_rows, channels),
            preferred_element_type=f32,
        )

    def forward_point(tile, preact):
        gate = jnp.where(tile_pos[tile] >= 0, 1.0, 0.0).astype(f32)
        cumulative = 0.5 * (1.0 + lax.erf(preact * ROOT_HALF))
        density = jnp.exp(-0.5 * preact * preact) * INV_ROOT_TAU
        act[tile] = (preact * cumulative * gate).astype(bf16).reshape(side, side, channels)
        grad = grad_out[tile].reshape(cells, channels).astype(f32)
        slope = grad * (cumulative + preact * density) * gate
        pre_grad[tile] = slope.astype(bf16).reshape(side, side, channels)
        pre_grad_t[tile] = slope.T.astype(bf16)

    batch = GROUP if tiles % GROUP == 0 else 1

    @pl.loop(0, tiles // batch)
    def _(turn):
        group = [turn * batch + at for at in range(batch)]
        preacts = [forward_dot(tile) for tile in group]
        for tile, preact in zip(group, preacts):
            forward_point(tile, preact)

    start_halo(1, pre_grad, above_g, below_g)

    def core_copy(k):
        return send(core_out.at[k], core_in.at[k], core_sems.at[0, k], core_peer)

    def near_copy(k):
        return send(near_out.at[k], near_in.at[k], near_sems.at[0, k], near_peer)

    def fan_copy(k, step):
        return send(
            fan_out.at[k, step - 1],
            fan_in.at[k, step - 1],
            fan_sems.at[0, k, step - 1],
            fan_peer(step),
        )

    def far_copy(k, turn):
        return send(far_out.at[k, turn], far_in.at[k, turn], far_sems.at[k, turn], far_peer(turn))

    def fan_back(k, step, owner):
        block = total.at[k, core, near, owner]
        return send(block, block, fan_sems.at[1, k, step - 1], fan_peer(step))

    def near_back(k, owner):
        block = total.at[k, core, owner]
        return send(block, block, near_sems.at[1, k], near_peer)

    def core_back(k, owner):
        block = total.at[k, owner]
        return send(block, block, core_sems.at[1, k], core_peer)

    def put_g(tile):
        def put(shift, rows, value):
            ext_g[shift, tile, rows] = value

        return put

    chunks = part.shape[0]
    width = taps // chunks

    def due(step, lag):
        since = step - lag - (width - 1)
        return (since >= 0) & (since < taps) & (lax.rem(since, width) == 0)

    def chunk_of(step, lag):
        return (step - lag - (width - 1)) // width

    @pl.loop(0, taps + LAG_CORE_BACK)
    def _(step):
        @pl.when(step < taps)
        def _():
            k = step
            rows = ext_x[lax.rem(k, 3), :, pl.ds(k // 3, side)].reshape(tiles * cells, channels)
            lhs = jnp.concatenate([pre_grad_t[tile] for tile in range(tiles)], axis=1)
            term = jnp.dot(lhs, rows, preferred_element_type=f32)
            chunk, at = k // width, lax.rem(k, width)
            part[chunk, :, :, :, at] = term.T.reshape(part.shape[1:4] + part.shape[5:])
            core_out[chunk, :, :, at] = part[chunk, 1 - core, :, :, at].astype(bf16)

            @pl.when(at == width - 1)
            def _():
                core_copy(chunk).start()


        @pl.when(due(step, LAG_CORE))
        def _():
            k = chunk_of(step, LAG_CORE)
            core_copy(k).wait_recv()
            part[k, core] = part[k, core] + core_in[k].astype(f32)
            near_out[k] = part[k, core, 1 - near].astype(bf16)
            near_copy(k).start()

        @pl.when(due(step, LAG_NEAR))
        def _():
            k = chunk_of(step, LAG_NEAR)
            near_copy(k).wait_recv()
            part[k, core, near] = part[k, core, near] + near_in[k].astype(f32)
            for turn in range(1, FAN):
                fan_out[k, turn - 1] = part[k, core, near, fan_slot(turn)].astype(bf16)
                fan_copy(k, turn).start()

        @pl.when(due(step, LAG_FAN))
        def _():
            k = chunk_of(step, LAG_FAN)
            sums = part[k, core, near, fan]
            for turn in range(1, FAN):
                fan_copy(k, turn).wait_recv()
                sums = sums + fan_in[k, turn - 1].astype(f32)
            for turn in range(far_rounds):
                far_out[k, turn] = sums.astype(bf16)
                copy = far_copy(k, turn)
                copy.start()
                copy.wait()
                sums = far_out[k, turn].astype(f32) + far_in[k, turn].astype(f32)
            total[k, core, near, fan] = (sums * scale).astype(bf16)
            for turn in range(1, FAN):
                fan_back(k, turn, fan).start()

        @pl.when(due(step, LAG_FAN_BACK))
        def _():
            k = chunk_of(step, LAG_FAN_BACK)
            for turn in range(1, FAN):
                fan_back(k, turn, fan_slot(-turn)).wait_recv()
            near_back(k, near).start()

        @pl.when(due(step, LAG_NEAR_BACK))
        def _():
            k = chunk_of(step, LAG_NEAR_BACK)
            near_back(k, 1 - near).wait_recv()
            core_back(k, core).start()

        @pl.when(due(step, LAG_CORE_BACK))
        def _():
            k = chunk_of(step, LAG_CORE_BACK)
            core_back(k, 1 - core).wait_recv()
            core_copy(k).wait_send()
            near_copy(k).wait_send()
            for turn in range(1, FAN):
                fan_copy(k, turn).wait_send()
                fan_back(k, turn, fan).wait_send()
            near_back(k, near).wait_send()
            core_back(k, core).wait_send()

        @pl.when(step == taps)
        def _():
            wait_halo(1, above_g, below_g)
            for tile in range(tiles):
                both_borders(above_g, below_g, tile, put_g(tile))

        @pl.when((step >= taps) & (step < taps + 3))
        def _():
            for at in range(taps // 3):
                tap = (step - taps) * (taps // 3) + at
                weights_t[tap] = weights[tap].astype(f32).T.astype(bf16)
            for at in range(tiles // 3):
                tile = (step - taps) * (tiles // 3) + at
                inner_rows(pre_grad, tile, put_g(tile))

        @pl.when((step >= taps + 3) & (step < taps + 3 + tiles))
        def _():
            tile = step - taps - 3
            pieces = [
                ext_g[2 - b, tile, 2 - a : 2 - a + side].reshape(cells, channels)
                for a in range(3)
                for b in range(3)
            ]
            back = jnp.dot(
                jnp.concatenate(pieces, axis=1),
                weights_t[...].reshape(weight_mat_rows, channels),
                preferred_element_type=f32,
            )
            gate = jnp.where(tile_pos[tile] >= 0, 1.0, 0.0).astype(f32)
            input_grad[tile] = (back * gate).astype(bf16).reshape(side, side, channels)


def finish(act_in, grad_in, back_in, act_out, grad_out, back_out, wide, sems):
    taps = wide.shape[0]
    copies = [
        pltpu.make_async_copy(back_in, back_out, sems.at[0]),
        pltpu.make_async_copy(act_in, act_out, sems.at[1]),
    ]
    for copy in copies:
        copy.start()
    chunks, width = grad_in.shape[0], grad_in.shape[4]
    for chunk in range(chunks):
        for at in range(width):
            block = grad_in[chunk, :, :, :, at].astype(jnp.float32)
            wide[chunk * width + at] = block.reshape(wide.shape[1:])
        rows = pl.ds(chunk * width, width)
        copies.append(pltpu.make_async_copy(wide.at[rows], grad_out.at[rows], sems.at[len(copies)]))
        copies[-1].start()
    for copy in copies:
        copy.wait()


def body(count, features, weights, grad_out, tile_pos, neighbours):
    bf16, f32 = jnp.bfloat16, jnp.float32
    tiles, side, _, channels = features.shape
    taps = weights.shape[0]
    scale = 1.0 / math.sqrt(tiles * count * side * side)
    chunks = taps // CHUNK
    split = (2, 2, FAN, CHUNK, channels // (4 * FAN), channels)
    far_rounds = int(math.log2(count // (4 * FAN)))
    table = pltpu.VMEM((2 * tiles + 1, side, channels), bf16)
    dma = pltpu.SemaphoreType.DMA
    hbm = pl.BlockSpec(memory_space=pl.ANY)
    vmem = pl.BlockSpec(memory_space=pltpu.VMEM)
    flops = 3 * 2 * tiles * side * side * taps * channels * channels
    act, grad_sum, input_grad = pl.pallas_call(
        functools.partial(kernel, count, scale),
        out_shape=(
            pltpu.VMEM(features.shape, bf16),
            pltpu.VMEM((chunks,) + split, bf16),
            pltpu.VMEM(features.shape, bf16),
        ),
        in_specs=[hbm] * 5,
        out_specs=(vmem, vmem, vmem),
        scratch_shapes=[
            pltpu.VMEM(features.shape, bf16),
            pltpu.VMEM(weights.shape, bf16),
            pltpu.VMEM(features.shape, bf16),
            pltpu.SMEM(tile_pos.shape, jnp.int32),
            pltpu.SMEM(neighbours.shape, jnp.int32),
            pltpu.VMEM((3, tiles, side + 2, side, channels), bf16),
            pltpu.VMEM((3, tiles, side + 2, side, channels), bf16),
            table,
            table,
            table,
            table,
            pltpu.VMEM((2, 2, tiles, side, channels), bf16),
            pltpu.VMEM(features.shape, bf16),
            pltpu.VMEM((tiles, channels, side * side), bf16),
            pltpu.VMEM(weights.shape, bf16),
            pltpu.VMEM((chunks,) + split, f32),
            pltpu.VMEM((chunks,) + split[1:], bf16),
            pltpu.VMEM((chunks,) + split[1:], bf16),
            pltpu.VMEM((chunks,) + split[2:], bf16),
            pltpu.VMEM((chunks,) + split[2:], bf16),
            pltpu.VMEM((chunks, FAN - 1) + split[3:], bf16),
            pltpu.VMEM((chunks, FAN - 1) + split[3:], bf16),
            pltpu.VMEM((chunks, far_rounds) + split[3:], bf16),
            pltpu.VMEM((chunks, far_rounds) + split[3:], bf16),
            dma((2, 2, 2)),
            dma((2, chunks, 2)),
            dma((2, chunks, 2)),
            dma((2, chunks, FAN - 1, 2)),
            dma((chunks, far_rounds, 2)),
            dma((5,)),
        ],
        compiler_params=pltpu.CompilerParams(
            collective_id=0, has_side_effects=True, vmem_limit_bytes=60 * 2**20
        ),
        cost_estimate=pl.CostEstimate(flops=flops, bytes_accessed=2**23, transcendentals=0),
        name="tile_conv_step",
    )(features, weights, grad_out, tile_pos, neighbours)
    return pl.pallas_call(
        finish,
        out_shape=(
            jax.ShapeDtypeStruct(act.shape, bf16),
            jax.ShapeDtypeStruct(weights.shape, f32),
            jax.ShapeDtypeStruct(act.shape, bf16),
        ),
        in_specs=[vmem] * 3,
        out_specs=(hbm, hbm, hbm),
        scratch_shapes=[
            pltpu.VMEM(weights.shape, f32),
            dma((2 + chunks,)),
        ],
        compiler_params=pltpu.CompilerParams(vmem_limit_bytes=8 * 2**20),
        name="write_results",
    )(act, grad_sum, input_grad)


def solution(mesh):
    in_specs = (
        P(("groups", "tile"), None, None, None),
        P(),
        P(("groups", "tile"), None, None, None),
        P(("groups", "tile")),
        P(("groups", "tile"), None),
    )
    out_specs = (
        P(("groups", "tile"), None, None, None),
        P("groups", None, None),
        P(("groups", "tile"), None, None, None),
    )
    return jax.shard_map(
        functools.partial(body, mesh.shape["tile"]),
        mesh=mesh,
        in_specs=in_specs,
        out_specs=out_specs,
        check_vma=False,
    )
```

```python
import functools
import math

import jax
import jax.numpy as jnp
from jax import lax
from jax.experimental import pallas as pl
from jax.experimental.pallas import tpu as pltpu
from jax.sharding import PartitionSpec as P

ROOT_HALF = 0.7071067811865476
INV_ROOT_TAU = 0.3989422804014327
FAN = 4
GROUP = 6
CHUNK = 1
LAG_CORE, LAG_NEAR, LAG_FAN, LAG_FAN_BACK, LAG_NEAR_BACK, LAG_CORE_BACK = (2, 5, 8, 11, 14, 16)
MESH = pl.DeviceIdType.MESH


def shifted(center, left, right, axis):
    cell = lax.broadcasted_iota(jnp.int32, center.shape, axis)
    side = center.shape[axis]
    from_left = pltpu.roll(jnp.where(cell == side - 1, left, center), 1, axis)
    from_right = pltpu.roll(jnp.where(cell == 0, right, center), side - 1, axis)
    return from_left, from_right


def kernel(
    count,
    scale,
    features_hbm,
    weights_hbm,
    grad_out_hbm,
    tile_pos_hbm,
    links_hbm,
    act,
    total,
    input_grad,
    features,
    weights,
    grad_out,
    tile_pos,
    links,
    ext_x,
    ext_g,
    above_x,
    below_x,
    above_g,
    below_g,
    rows_out,
    pre_grad,
    pre_grad_t,
    weights_t,
    part,
    core_out,
    core_in,
    near_out,
    near_in,
    fan_out,
    fan_in,
    far_out,
    far_in,
    halo_sems,
    core_sems,
    near_sems,
    fan_sems,
    far_sems,
    load_sems,
):
    f32, bf16 = jnp.float32, jnp.bfloat16
    tiles, side, _, channels = features.shape
    cells = side * side
    taps = weights.shape[0]
    zero_row = 2 * tiles
    me = lax.axis_index("tile")
    core = lax.rem(me, 2)
    near = lax.rem(me // 2, 2)
    fan = lax.rem(me // 4, FAN)
    base = me - core - 2 * near - 4 * fan
    core_peer = me + 1 - 2 * core
    near_peer = me + 2 - 4 * near
    far_rounds = far_out.shape[1]

    def fan_slot(step):
        return lax.rem(fan + step + FAN, FAN)

    def fan_peer(step):
        return base + 4 * fan_slot(step) + 2 * near + core

    def far_peer(turn):
        stride = 4 * FAN * 2**turn
        return me + stride - 2 * stride * lax.rem(me // stride, 2)

    def send(source, target, sems, peer):
        return pltpu.make_async_remote_copy(
            src_ref=source,
            dst_ref=target,
            send_sem=sems.at[0],
            recv_sem=sems.at[1],
            device_id={"tile": peer},
            device_id_type=MESH,
        )

    pairs = (
        (features_hbm, features),
        (links_hbm, links),
        (weights_hbm, weights),
        (tile_pos_hbm, tile_pos),
        (grad_out_hbm, grad_out),
    )
    loads = [pltpu.make_async_copy(*pair, load_sems.at[at]) for at, pair in enumerate(pairs)]
    for load in loads:
        load.start()

    has_prev, has_next = me > 0, me < count - 1
    barrier = pltpu.get_barrier_semaphore()
    peers = [core_peer, near_peer] + [fan_peer(step) for step in range(1, FAN)]
    peers = peers + [far_peer(turn) for turn in range(far_rounds)]
    for peer in peers:
        pl.semaphore_signal(barrier, inc=1, device_id={"tile": peer}, device_id_type=MESH)

    @pl.when(has_prev)
    def _():
        pl.semaphore_signal(barrier, inc=1, device_id={"tile": me - 1}, device_id_type=MESH)

    @pl.when(has_next)
    def _():
        pl.semaphore_signal(barrier, inc=1, device_id={"tile": me + 1}, device_id_type=MESH)

    pl.semaphore_wait(barrier, len(peers) + jnp.where(has_prev, 1, 0) + jnp.where(has_next, 1, 0))

    def halo(turn, above, below):
        down = send(rows_out.at[turn, 0], above.at[pl.ds(0, tiles)], halo_sems.at[turn, 0], me + 1)
        up = send(rows_out.at[turn, 1], below.at[pl.ds(tiles, tiles)], halo_sems.at[turn, 1], me - 1)
        return down, up

    def start_halo(turn, field, above, below):
        last, first = field[:, side - 1], field[:, 0]
        rows_out[turn, 0] = last
        rows_out[turn, 1] = first
        down, up = halo(turn, above, below)

        @pl.when(has_next)
        def _():
            down.start()

        @pl.when(has_prev)
        def _():
            up.start()

        above[tiles : 2 * tiles] = last
        below[0:tiles] = first
        for table in (above, below):
            table[zero_row] = jnp.zeros(table.shape[1:], table.dtype)

    def wait_halo(turn, above, below):
        down, up = halo(turn, above, below)

        @pl.when(has_next)
        def _():
            down.wait_send()
            up.wait_recv()

        @pl.when(has_prev)
        def _():
            up.wait_send()
            down.wait_recv()

    def link_gate(code):
        return jnp.where(code >= 0, 1.0, 0.0).astype(f32)

    def inner_rows(field, tile, put):
        center = field[tile]
        left, right = links[tile, 2], links[tile, 3]
        left_map = field[jnp.where(left >= tiles, left - tiles, tile)].astype(f32) * link_gate(left)
        right_map = field[jnp.where(right >= tiles, right - tiles, tile)].astype(f32) * link_gate(right)
        from_left, from_right = shifted(center.astype(f32), left_map, right_map, 1)
        inner = slice(1, side + 1)
        put(0, inner, from_left.astype(bf16))
        put(1, inner, center)
        put(2, inner, from_right.astype(bf16))

    def border_rows(table, row, tile, first_link, left_link, right_link, base_code, put):
        def pick(link):
            code = links[tile, link]
            return table[jnp.where(code >= base_code, code - base_code, zero_row)]

        center = pick(first_link)
        from_left, from_right = shifted(
            center.astype(f32), pick(left_link).astype(f32), pick(right_link).astype(f32), 0
        )
        put(0, row, from_left.astype(bf16))
        put(1, row, center)
        put(2, row, from_right.astype(bf16))

    def both_borders(above, below, tile, put):
        border_rows(above, 0, tile, 0, 4, 5, 0, put)
        border_rows(below, side + 1, tile, 1, 6, 7, tiles, put)

    loads[0].wait()
    loads[1].wait()

    start_halo(0, features, above_x, below_x)

    def put_x(tile):
        def put(shift, rows, value):
            ext_x[shift, tile, rows] = value

        return put

    @pl.loop(0, tiles)
    def _(tile):
        inner_rows(features, tile, put_x(tile))

    wait_halo(0, above_x, below_x)

    for tile in range(tiles):
        both_borders(above_x, below_x, tile, put_x(tile))

    for load in loads[2:]:
        load.wait()

    weight_mat_rows = taps * channels

    def forward_dot(tile):
        pieces = [
            ext_x[b, tile, a : a + side].reshape(cells, channels) for a in range(3) for b in range(3)
        ]
        return jnp.dot(
            jnp.concatenate(pieces, axis=1),
            weights[...].reshape(weight_mat_rows, channels),
            preferred_element_type=f32,
        )

    def forward_point(tile, preact):
        gate = jnp.where(tile_pos[tile] >= 0, 1.0, 0.0).astype(f32)
        cumulative = 0.5 * (1.0 + lax.erf(preact * ROOT_HALF))
        density = jnp.exp(-0.5 * preact * preact) * INV_ROOT_TAU
        act[tile] = (preact * cumulative * gate).astype(bf16).reshape(side, side, channels)
        grad = grad_out[tile].reshape(cells, channels).astype(f32)
        slope = grad * (cumulative + preact * density) * gate
        pre_grad[tile] = slope.astype(bf16).reshape(side, side, channels)
        pre_grad_t[tile] = slope.T.astype(bf16)

    batch = GROUP if tiles % GROUP == 0 else 1

    @pl.loop(0, tiles // batch)
    def _(turn):
        group = [turn * batch + at for at in range(batch)]
        waiting = forward_dot(group[0])
        for at, tile in enumerate(group):
            preact = waiting
            if at + 1 < batch:
                waiting = forward_dot(group[at + 1])
            forward_point(tile, preact)

    start_halo(1, pre_grad, above_g, below_g)

    def core_copy(k):
        return send(core_out.at[k], core_in.at[k], core_sems.at[0, k], core_peer)

    def near_copy(k):
        return send(near_out.at[k], near_in.at[k], near_sems.at[0, k], near_peer)

    def fan_copy(k, step):
        return send(
            fan_out.at[k, step - 1],
            fan_in.at[k, step - 1],
            fan_sems.at[0, k, step - 1],
            fan_peer(step),
        )

    def far_copy(k, turn):
        return send(far_out.at[k, turn], far_in.at[k, turn], far_sems.at[k, turn], far_peer(turn))

    def fan_back(k, step, owner):
        block = total.at[k, core, near, owner]
        return send(block, block, fan_sems.at[1, k, step - 1], fan_peer(step))

    def near_back(k, owner):
        block = total.at[k, core, owner]
        return send(block, block, near_sems.at[1, k], near_peer)

    def core_back(k, owner):
        block = total.at[k, owner]
        return send(block, block, core_sems.at[1, k], core_peer)

    def put_g(tile):
        def put(shift, rows, value):
            ext_g[shift, tile, rows] = value

        return put

    chunks = part.shape[0]
    width = taps // chunks

    def due(step, lag):
        since = step - lag - (width - 1)
        return (since >= 0) & (since < taps) & (lax.rem(since, width) == 0)

    def chunk_of(step, lag):
        return (step - lag - (width - 1)) // width

    @pl.loop(0, taps + LAG_CORE_BACK)
    def _(step):
        @pl.when(step < taps)
        def _():
            k = step
            rows = ext_x[lax.rem(k, 3), :, pl.ds(k // 3, side)].reshape(tiles * cells, channels)
            lhs = jnp.concatenate([pre_grad_t[tile] for tile in range(tiles)], axis=1)
            term = jnp.dot(lhs, rows, preferred_element_type=f32)
            chunk, at = k // width, lax.rem(k, width)
            part[chunk, :, :, :, at] = term.T.reshape(part.shape[1:4] + part.shape[5:])
            core_out[chunk, :, :, at] = part[chunk, 1 - core, :, :, at].astype(bf16)

            @pl.when(at == width - 1)
            def _():
                core_copy(chunk).start()


        @pl.when(due(step, LAG_CORE))
        def _():
            k = chunk_of(step, LAG_CORE)
            core_copy(k).wait_recv()
            part[k, core] = part[k, core] + core_in[k].astype(f32)
            near_out[k] = part[k, core, 1 - near].astype(bf16)
            near_copy(k).start()

        @pl.when(due(step, LAG_NEAR))
        def _():
            k = chunk_of(step, LAG_NEAR)
            near_copy(k).wait_recv()
            part[k, core, near] = part[k, core, near] + near_in[k].astype(f32)
            for turn in range(1, FAN):
                fan_out[k, turn - 1] = part[k, core, near, fan_slot(turn)].astype(bf16)
                fan_copy(k, turn).start()

        @pl.when(due(step, LAG_FAN))
        def _():
            k = chunk_of(step, LAG_FAN)
            sums = part[k, core, near, fan]
            for turn in range(1, FAN):
                fan_copy(k, turn).wait_recv()
                sums = sums + fan_in[k, turn - 1].astype(f32)
            for turn in range(far_rounds):
                far_out[k, turn] = sums.astype(bf16)
                copy = far_copy(k, turn)
                copy.start()
                copy.wait()
                sums = far_out[k, turn].astype(f32) + far_in[k, turn].astype(f32)
            total[k, core, near, fan] = (sums * scale).astype(bf16)
            for turn in range(1, FAN):
                fan_back(k, turn, fan).start()

        @pl.when(due(step, LAG_FAN_BACK))
        def _():
            k = chunk_of(step, LAG_FAN_BACK)
            for turn in range(1, FAN):
                fan_back(k, turn, fan_slot(-turn)).wait_recv()
            near_back(k, near).start()

        @pl.when(due(step, LAG_NEAR_BACK))
        def _():
            k = chunk_of(step, LAG_NEAR_BACK)
            near_back(k, 1 - near).wait_recv()
            core_back(k, core).start()

        @pl.when(due(step, LAG_CORE_BACK))
        def _():
            k = chunk_of(step, LAG_CORE_BACK)
            core_back(k, 1 - core).wait_recv()
            core_copy(k).wait_send()
            near_copy(k).wait_send()
            for turn in range(1, FAN):
                fan_copy(k, turn).wait_send()
                fan_back(k, turn, fan).wait_send()
            near_back(k, near).wait_send()
            core_back(k, core).wait_send()

        @pl.when(step == taps)
        def _():
            wait_halo(1, above_g, below_g)
            for tile in range(tiles):
                both_borders(above_g, below_g, tile, put_g(tile))

        turn = step - taps
        unit = (turn // 3) * 2 + lax.rem(turn, 3)
        working = (turn >= 0) & (lax.rem(turn, 3) < 2)

        @pl.when(working & (unit < 3))
        def _():
            for at in range(taps // 3):
                tap = unit * (taps // 3) + at
                weights_t[tap] = weights[tap].astype(f32).T.astype(bf16)
            for at in range(tiles // 3):
                tile = unit * (tiles // 3) + at
                inner_rows(pre_grad, tile, put_g(tile))

        @pl.when(working & (unit >= 3) & (unit < 3 + tiles))
        def _():
            tile = unit - 3
            pieces = [
                ext_g[2 - b, tile, 2 - a : 2 - a + side].reshape(cells, channels)
                for a in range(3)
                for b in range(3)
            ]
            back = jnp.dot(
                jnp.concatenate(pieces, axis=1),
                weights_t[...].reshape(weight_mat_rows, channels),
                preferred_element_type=f32,
            )
            gate = jnp.where(tile_pos[tile] >= 0, 1.0, 0.0).astype(f32)
            input_grad[tile] = (back * gate).astype(bf16).reshape(side, side, channels)


def finish(act_in, grad_in, back_in, act_out, grad_out, back_out, wide, sems):
    taps = wide.shape[0]
    copies = [
        pltpu.make_async_copy(back_in, back_out, sems.at[0]),
        pltpu.make_async_copy(act_in, act_out, sems.at[1]),
    ]
    for copy in copies:
        copy.start()
    chunks, width = grad_in.shape[0], grad_in.shape[4]
    for chunk in range(chunks):
        for at in range(width):
            block = grad_in[chunk, :, :, :, at].astype(jnp.float32)
            wide[chunk * width + at] = block.reshape(wide.shape[1:])
        rows = pl.ds(chunk * width, width)
        copies.append(pltpu.make_async_copy(wide.at[rows], grad_out.at[rows], sems.at[len(copies)]))
        copies[-1].start()
    for copy in copies:
        copy.wait()


def body(count, features, weights, grad_out, tile_pos, neighbours):
    bf16, f32 = jnp.bfloat16, jnp.float32
    tiles, side, _, channels = features.shape
    taps = weights.shape[0]
    scale = 1.0 / math.sqrt(tiles * count * side * side)
    chunks = taps // CHUNK
    split = (2, 2, FAN, CHUNK, channels // (4 * FAN), channels)
    far_rounds = int(math.log2(count // (4 * FAN)))
    table = pltpu.VMEM((2 * tiles + 1, side, channels), bf16)
    dma = pltpu.SemaphoreType.DMA
    hbm = pl.BlockSpec(memory_space=pl.ANY)
    vmem = pl.BlockSpec(memory_space=pltpu.VMEM)
    flops = 3 * 2 * tiles * side * side * taps * channels * channels
    act, grad_sum, input_grad = pl.pallas_call(
        functools.partial(kernel, count, scale),
        out_shape=(
            pltpu.VMEM(features.shape, bf16),
            pltpu.VMEM((chunks,) + split, bf16),
            pltpu.VMEM(features.shape, bf16),
        ),
        in_specs=[hbm] * 5,
        out_specs=(vmem, vmem, vmem),
        scratch_shapes=[
            pltpu.VMEM(features.shape, bf16),
            pltpu.VMEM(weights.shape, bf16),
            pltpu.VMEM(features.shape, bf16),
            pltpu.SMEM(tile_pos.shape, jnp.int32),
            pltpu.SMEM(neighbours.shape, jnp.int32),
            pltpu.VMEM((3, tiles, side + 2, side, channels), bf16),
            pltpu.VMEM((3, tiles, side + 2, side, channels), bf16),
            table,
            table,
            table,
            table,
            pltpu.VMEM((2, 2, tiles, side, channels), bf16),
            pltpu.VMEM(features.shape, bf16),
            pltpu.VMEM((tiles, channels, side * side), bf16),
            pltpu.VMEM(weights.shape, bf16),
            pltpu.VMEM((chunks,) + split, f32),
            pltpu.VMEM((chunks,) + split[1:], bf16),
            pltpu.VMEM((chunks,) + split[1:], bf16),
            pltpu.VMEM((chunks,) + split[2:], bf16),
            pltpu.VMEM((chunks,) + split[2:], bf16),
            pltpu.VMEM((chunks, FAN - 1) + split[3:], bf16),
            pltpu.VMEM((chunks, FAN - 1) + split[3:], bf16),
            pltpu.VMEM((chunks, far_rounds) + split[3:], bf16),
            pltpu.VMEM((chunks, far_rounds) + split[3:], bf16),
            dma((2, 2, 2)),
            dma((2, chunks, 2)),
            dma((2, chunks, 2)),
            dma((2, chunks, FAN - 1, 2)),
            dma((chunks, far_rounds, 2)),
            dma((5,)),
        ],
        compiler_params=pltpu.CompilerParams(
            collective_id=0, has_side_effects=True, vmem_limit_bytes=60 * 2**20
        ),
        cost_estimate=pl.CostEstimate(flops=flops, bytes_accessed=2**23, transcendentals=0),
        name="tile_conv_step",
    )(features, weights, grad_out, tile_pos, neighbours)
    return pl.pallas_call(
        finish,
        out_shape=(
            jax.ShapeDtypeStruct(act.shape, bf16),
            jax.ShapeDtypeStruct(weights.shape, f32),
            jax.ShapeDtypeStruct(act.shape, bf16),
        ),
        in_specs=[vmem] * 3,
        out_specs=(hbm, hbm, hbm),
        scratch_shapes=[
            pltpu.VMEM(weights.shape, f32),
            dma((2 + chunks,)),
        ],
        compiler_params=pltpu.CompilerParams(vmem_limit_bytes=8 * 2**20),
        name="write_results",
    )(act, grad_sum, input_grad)


def solution(mesh):
    in_specs = (
        P(("groups", "tile"), None, None, None),
        P(),
        P(("groups", "tile"), None, None, None),
        P(("groups", "tile")),
        P(("groups", "tile"), None),
    )
    out_specs = (
        P(("groups", "tile"), None, None, None),
        P("groups", None, None),
        P(("groups", "tile"), None, None, None),
    )
    return jax.shard_map(
        functools.partial(body, mesh.shape["tile"]),
        mesh=mesh,
        in_specs=in_specs,
        out_specs=out_specs,
        check_vma=False,
    )
```

```python
import functools
import math

import jax
import jax.numpy as jnp
from jax import lax
from jax.experimental import pallas as pl
from jax.experimental.pallas import tpu as pltpu
from jax.sharding import PartitionSpec as P

ROOT_HALF = 0.7071067811865476
INV_ROOT_TAU = 0.3989422804014327
FAN = 4
GROUP = 6
CHUNK = 1
LAG_CORE, LAG_NEAR, LAG_FAN, LAG_FAN_BACK, LAG_NEAR_BACK, LAG_CORE_BACK = (3, 6, 9, 11, 13, 14)
MESH = pl.DeviceIdType.MESH


def shifted(center, left, right, axis):
    cell = lax.broadcasted_iota(jnp.int32, center.shape, axis)
    side = center.shape[axis]
    from_left = pltpu.roll(jnp.where(cell == side - 1, left, center), 1, axis)
    from_right = pltpu.roll(jnp.where(cell == 0, right, center), side - 1, axis)
    return from_left, from_right


def kernel(
    count,
    scale,
    features_hbm,
    weights_hbm,
    grad_out_hbm,
    tile_pos_hbm,
    links_hbm,
    act,
    total,
    input_grad,
    features,
    weights,
    grad_out,
    tile_pos,
    links,
    ext_x,
    ext_g,
    above_x,
    below_x,
    above_g,
    below_g,
    rows_out,
    pre_grad,
    pre_grad_t,
    weights_t,
    part,
    term,
    core_out,
    core_in,
    near_out,
    near_in,
    fan_out,
    fan_in,
    far_out,
    far_in,
    halo_sems,
    core_sems,
    near_sems,
    fan_sems,
    far_sems,
    load_sems,
):
    f32, bf16 = jnp.float32, jnp.bfloat16
    tiles, side, _, channels = features.shape
    cells = side * side
    taps = weights.shape[0]
    zero_row = 2 * tiles
    me = lax.axis_index("tile")
    core = lax.rem(me, 2)
    near = lax.rem(me // 2, 2)
    fan = lax.rem(me // 4, FAN)
    base = me - core - 2 * near - 4 * fan
    core_peer = me + 1 - 2 * core
    near_peer = me + 2 - 4 * near
    far_rounds = far_out.shape[1]

    def fan_slot(step):
        return lax.rem(fan + step + FAN, FAN)

    def fan_peer(step):
        return base + 4 * fan_slot(step) + 2 * near + core

    def far_peer(turn):
        stride = 4 * FAN * 2**turn
        return me + stride - 2 * stride * lax.rem(me // stride, 2)

    def send(source, target, sems, peer):
        return pltpu.make_async_remote_copy(
            src_ref=source,
            dst_ref=target,
            send_sem=sems.at[0],
            recv_sem=sems.at[1],
            device_id={"tile": peer},
            device_id_type=MESH,
        )

    pairs = (
        (features_hbm, features),
        (links_hbm, links),
        (weights_hbm, weights),
        (tile_pos_hbm, tile_pos),
        (grad_out_hbm, grad_out),
    )
    loads = [pltpu.make_async_copy(*pair, load_sems.at[at]) for at, pair in enumerate(pairs)]
    for load in loads:
        load.start()

    has_prev, has_next = me > 0, me < count - 1
    barrier = pltpu.get_barrier_semaphore()
    peers = [core_peer, near_peer] + [fan_peer(step) for step in range(1, FAN)]
    peers = peers + [far_peer(turn) for turn in range(far_rounds)]
    for peer in peers:
        pl.semaphore_signal(barrier, inc=1, device_id={"tile": peer}, device_id_type=MESH)

    @pl.when(has_prev)
    def _():
        pl.semaphore_signal(barrier, inc=1, device_id={"tile": me - 1}, device_id_type=MESH)

    @pl.when(has_next)
    def _():
        pl.semaphore_signal(barrier, inc=1, device_id={"tile": me + 1}, device_id_type=MESH)

    pl.semaphore_wait(barrier, len(peers) + jnp.where(has_prev, 1, 0) + jnp.where(has_next, 1, 0))

    def halo(turn, above, below):
        down = send(rows_out.at[turn, 0], above.at[pl.ds(0, tiles)], halo_sems.at[turn, 0], me + 1)
        up = send(rows_out.at[turn, 1], below.at[pl.ds(tiles, tiles)], halo_sems.at[turn, 1], me - 1)
        return down, up

    def start_halo(turn, field, above, below):
        last, first = field[:, side - 1], field[:, 0]
        rows_out[turn, 0] = last
        rows_out[turn, 1] = first
        down, up = halo(turn, above, below)

        @pl.when(has_next)
        def _():
            down.start()

        @pl.when(has_prev)
        def _():
            up.start()

        above[tiles : 2 * tiles] = last
        below[0:tiles] = first
        for table in (above, below):
            table[zero_row] = jnp.zeros(table.shape[1:], table.dtype)

    def wait_halo(turn, above, below):
        down, up = halo(turn, above, below)

        @pl.when(has_next)
        def _():
            down.wait_send()
            up.wait_recv()

        @pl.when(has_prev)
        def _():
            up.wait_send()
            down.wait_recv()

    def link_gate(code):
        return jnp.where(code >= 0, 1.0, 0.0).astype(f32)

    def inner_rows(field, tile, put):
        center = field[tile]
        left, right = links[tile, 2], links[tile, 3]
        left_map = field[jnp.where(left >= tiles, left - tiles, tile)].astype(f32) * link_gate(left)
        right_map = field[jnp.where(right >= tiles, right - tiles, tile)].astype(f32) * link_gate(right)
        from_left, from_right = shifted(center.astype(f32), left_map, right_map, 1)
        inner = slice(1, side + 1)
        put(0, inner, from_left.astype(bf16))
        put(1, inner, center)
        put(2, inner, from_right.astype(bf16))

    def border_rows(table, row, tile, first_link, left_link, right_link, base_code, put):
        def pick(link):
            code = links[tile, link]
            return table[jnp.where(code >= base_code, code - base_code, zero_row)]

        center = pick(first_link)
        from_left, from_right = shifted(
            center.astype(f32), pick(left_link).astype(f32), pick(right_link).astype(f32), 0
        )
        put(0, row, from_left.astype(bf16))
        put(1, row, center)
        put(2, row, from_right.astype(bf16))

    def both_borders(above, below, tile, put):
        border_rows(above, 0, tile, 0, 4, 5, 0, put)
        border_rows(below, side + 1, tile, 1, 6, 7, tiles, put)

    loads[0].wait()
    loads[1].wait()

    start_halo(0, features, above_x, below_x)

    def put_x(tile):
        def put(shift, rows, value):
            ext_x[shift, tile, rows] = value

        return put

    @pl.loop(0, tiles)
    def _(tile):
        inner_rows(features, tile, put_x(tile))

    wait_halo(0, above_x, below_x)

    for tile in range(tiles):
        both_borders(above_x, below_x, tile, put_x(tile))

    for load in loads[2:]:
        load.wait()

    weight_mat_rows = taps * channels

    def forward_dot(tile):
        pieces = [
            ext_x[b, tile, a : a + side].reshape(cells, channels) for a in range(3) for b in range(3)
        ]
        return jnp.dot(
            jnp.concatenate(pieces, axis=1),
            weights[...].reshape(weight_mat_rows, channels),
            preferred_element_type=f32,
        )

    def forward_point(tile, preact):
        gate = jnp.where(tile_pos[tile] >= 0, 1.0, 0.0).astype(f32)
        cumulative = 0.5 * (1.0 + lax.erf(preact * ROOT_HALF))
        density = jnp.exp(-0.5 * preact * preact) * INV_ROOT_TAU
        act[tile] = (preact * cumulative * gate).astype(bf16).reshape(side, side, channels)
        grad = grad_out[tile].reshape(cells, channels).astype(f32)
        slope = grad * (cumulative + preact * density) * gate
        pre_grad[tile] = slope.astype(bf16).reshape(side, side, channels)
        pre_grad_t[tile] = slope.T.astype(bf16)

    batch = GROUP if tiles % GROUP == 0 else 1

    @pl.loop(0, tiles // batch)
    def _(turn):
        group = [turn * batch + at for at in range(batch)]
        waiting = forward_dot(group[0])
        for at, tile in enumerate(group):
            preact = waiting
            if at + 1 < batch:
                waiting = forward_dot(group[at + 1])
            forward_point(tile, preact)

    start_halo(1, pre_grad, above_g, below_g)

    def core_copy(k):
        return send(core_out.at[k], core_in.at[k], core_sems.at[0, k], core_peer)

    def near_copy(k):
        return send(near_out.at[k], near_in.at[k], near_sems.at[0, k], near_peer)

    def fan_copy(k, step):
        return send(
            fan_out.at[k, step - 1],
            fan_in.at[k, step - 1],
            fan_sems.at[0, k, step - 1],
            fan_peer(step),
        )

    def far_copy(k, turn):
        return send(far_out.at[k, turn], far_in.at[k, turn], far_sems.at[k, turn], far_peer(turn))

    def fan_back(k, step, owner):
        block = total.at[k, core, near, owner]
        return send(block, block, fan_sems.at[1, k, step - 1], fan_peer(step))

    def near_back(k, owner):
        block = total.at[k, core, owner]
        return send(block, block, near_sems.at[1, k], near_peer)

    def core_back(k, owner):
        block = total.at[k, owner]
        return send(block, block, core_sems.at[1, k], core_peer)

    def put_g(tile):
        def put(shift, rows, value):
            ext_g[shift, tile, rows] = value

        return put

    chunks = part.shape[0]
    width = taps // chunks

    def due(step, lag):
        since = step - lag - (width - 1)
        return (since >= 0) & (since < taps) & (lax.rem(since, width) == 0)

    def chunk_of(step, lag):
        return (step - lag - (width - 1)) // width

    @pl.loop(0, taps + LAG_CORE_BACK)
    def _(step):
        def hand_over(tap):
            chunk, at = tap // width, lax.rem(tap, width)
            part[chunk, :, :, :, at] = term[...].T.reshape(part.shape[1:4] + part.shape[5:])
            core_out[chunk, :, :, at] = part[chunk, 1 - core, :, :, at].astype(bf16)

        @pl.when(step < taps)
        def _():
            hand_over(jnp.maximum(step - 1, 0))
            rows = ext_x[lax.rem(step, 3), :, pl.ds(step // 3, side)]
            lhs = jnp.concatenate([pre_grad_t[tile] for tile in range(tiles)], axis=1)
            term[...] = jnp.dot(
                lhs, rows.reshape(tiles * cells, channels), preferred_element_type=f32
            )

        @pl.when(step == taps)
        def _():
            hand_over(taps - 1)

        @pl.when((step >= 1) & (step <= taps) & (lax.rem(step, width) == 0))
        def _():
            core_copy((step - 1) // width).start()

        @pl.when(due(step, LAG_CORE))
        def _():
            k = chunk_of(step, LAG_CORE)
            core_copy(k).wait_recv()
            part[k, core] = part[k, core] + core_in[k].astype(f32)
            near_out[k] = part[k, core, 1 - near].astype(bf16)
            near_copy(k).start()

        @pl.when(due(step, LAG_NEAR))
        def _():
            k = chunk_of(step, LAG_NEAR)
            near_copy(k).wait_recv()
            part[k, core, near] = part[k, core, near] + near_in[k].astype(f32)
            for turn in range(1, FAN):
                fan_out[k, turn - 1] = part[k, core, near, fan_slot(turn)].astype(bf16)
                fan_copy(k, turn).start()

        @pl.when(due(step, LAG_FAN))
        def _():
            k = chunk_of(step, LAG_FAN)
            sums = part[k, core, near, fan]
            for turn in range(1, FAN):
                fan_copy(k, turn).wait_recv()
                sums = sums + fan_in[k, turn - 1].astype(f32)
            for turn in range(far_rounds):
                far_out[k, turn] = sums.astype(bf16)
                copy = far_copy(k, turn)
                copy.start()
                copy.wait()
                sums = far_out[k, turn].astype(f32) + far_in[k, turn].astype(f32)
            total[k, core, near, fan] = (sums * scale).astype(bf16)
            for turn in range(1, FAN):
                fan_back(k, turn, fan).start()

        @pl.when(due(step, LAG_FAN_BACK))
        def _():
            k = chunk_of(step, LAG_FAN_BACK)
            for turn in range(1, FAN):
                fan_back(k, turn, fan_slot(-turn)).wait_recv()
            near_back(k, near).start()

        @pl.when(due(step, LAG_NEAR_BACK))
        def _():
            k = chunk_of(step, LAG_NEAR_BACK)
            near_back(k, 1 - near).wait_recv()
            core_back(k, core).start()

        @pl.when(due(step, LAG_CORE_BACK))
        def _():
            k = chunk_of(step, LAG_CORE_BACK)
            core_back(k, 1 - core).wait_recv()
            core_copy(k).wait_send()
            near_copy(k).wait_send()
            for turn in range(1, FAN):
                fan_copy(k, turn).wait_send()
                fan_back(k, turn, fan).wait_send()
            near_back(k, near).wait_send()
            core_back(k, core).wait_send()

        @pl.when(step == taps)
        def _():
            wait_halo(1, above_g, below_g)
            for tile in range(tiles):
                both_borders(above_g, below_g, tile, put_g(tile))

        turn = step - taps
        unit = (turn // 3) * 2 + lax.rem(turn, 3)
        working = (turn >= 0) & (lax.rem(turn, 3) < 2)

        @pl.when(working & (unit < 3))
        def _():
            for at in range(taps // 3):
                tap = unit * (taps // 3) + at
                weights_t[tap] = weights[tap].astype(f32).T.astype(bf16)
            for at in range(tiles // 3):
                tile = unit * (tiles // 3) + at
                inner_rows(pre_grad, tile, put_g(tile))

        @pl.when(working & (unit >= 3) & (unit < 3 + tiles))
        def _():
            tile = unit - 3
            pieces = [
                ext_g[2 - b, tile, 2 - a : 2 - a + side].reshape(cells, channels)
                for a in range(3)
                for b in range(3)
            ]
            back = jnp.dot(
                jnp.concatenate(pieces, axis=1),
                weights_t[...].reshape(weight_mat_rows, channels),
                preferred_element_type=f32,
            )
            gate = jnp.where(tile_pos[tile] >= 0, 1.0, 0.0).astype(f32)
            input_grad[tile] = (back * gate).astype(bf16).reshape(side, side, channels)


def finish(act_in, grad_in, back_in, act_out, grad_out, back_out, wide, sems):
    taps = wide.shape[0]
    copies = [
        pltpu.make_async_copy(back_in, back_out, sems.at[0]),
        pltpu.make_async_copy(act_in, act_out, sems.at[1]),
    ]
    for copy in copies:
        copy.start()
    chunks, width = grad_in.shape[0], grad_in.shape[4]
    for chunk in range(chunks):
        for at in range(width):
            block = grad_in[chunk, :, :, :, at].astype(jnp.float32)
            wide[chunk * width + at] = block.reshape(wide.shape[1:])
        rows = pl.ds(chunk * width, width)
        copies.append(pltpu.make_async_copy(wide.at[rows], grad_out.at[rows], sems.at[len(copies)]))
        copies[-1].start()
    for copy in copies:
        copy.wait()


def body(count, features, weights, grad_out, tile_pos, neighbours):
    bf16, f32 = jnp.bfloat16, jnp.float32
    tiles, side, _, channels = features.shape
    taps = weights.shape[0]
    scale = 1.0 / math.sqrt(tiles * count * side * side)
    chunks = taps // CHUNK
    split = (2, 2, FAN, CHUNK, channels // (4 * FAN), channels)
    far_rounds = int(math.log2(count // (4 * FAN)))
    table = pltpu.VMEM((2 * tiles + 1, side, channels), bf16)
    dma = pltpu.SemaphoreType.DMA
    hbm = pl.BlockSpec(memory_space=pl.ANY)
    vmem = pl.BlockSpec(memory_space=pltpu.VMEM)
    flops = 3 * 2 * tiles * side * side * taps * channels * channels
    act, grad_sum, input_grad = pl.pallas_call(
        functools.partial(kernel, count, scale),
        out_shape=(
            pltpu.VMEM(features.shape, bf16),
            pltpu.VMEM((chunks,) + split, bf16),
            pltpu.VMEM(features.shape, bf16),
        ),
        in_specs=[hbm] * 5,
        out_specs=(vmem, vmem, vmem),
        scratch_shapes=[
            pltpu.VMEM(features.shape, bf16),
            pltpu.VMEM(weights.shape, bf16),
            pltpu.VMEM(features.shape, bf16),
            pltpu.SMEM(tile_pos.shape, jnp.int32),
            pltpu.SMEM(neighbours.shape, jnp.int32),
            pltpu.VMEM((3, tiles, side + 2, side, channels), bf16),
            pltpu.VMEM((3, tiles, side + 2, side, channels), bf16),
            table,
            table,
            table,
            table,
            pltpu.VMEM((2, 2, tiles, side, channels), bf16),
            pltpu.VMEM(features.shape, bf16),
            pltpu.VMEM((tiles, channels, side * side), bf16),
            pltpu.VMEM(weights.shape, bf16),
            pltpu.VMEM((chunks,) + split, f32),
            pltpu.VMEM((channels, channels), f32),
            pltpu.VMEM((chunks,) + split[1:], bf16),
            pltpu.VMEM((chunks,) + split[1:], bf16),
            pltpu.VMEM((chunks,) + split[2:], bf16),
            pltpu.VMEM((chunks,) + split[2:], bf16),
            pltpu.VMEM((chunks, FAN - 1) + split[3:], bf16),
            pltpu.VMEM((chunks, FAN - 1) + split[3:], bf16),
            pltpu.VMEM((chunks, far_rounds) + split[3:], bf16),
            pltpu.VMEM((chunks, far_rounds) + split[3:], bf16),
            dma((2, 2, 2)),
            dma((2, chunks, 2)),
            dma((2, chunks, 2)),
            dma((2, chunks, FAN - 1, 2)),
            dma((chunks, far_rounds, 2)),
            dma((5,)),
        ],
        compiler_params=pltpu.CompilerParams(
            collective_id=0, has_side_effects=True, vmem_limit_bytes=60 * 2**20
        ),
        cost_estimate=pl.CostEstimate(flops=flops, bytes_accessed=2**23, transcendentals=0),
        name="tile_conv_step",
    )(features, weights, grad_out, tile_pos, neighbours)
    return pl.pallas_call(
        finish,
        out_shape=(
            jax.ShapeDtypeStruct(act.shape, bf16),
            jax.ShapeDtypeStruct(weights.shape, f32),
            jax.ShapeDtypeStruct(act.shape, bf16),
        ),
        in_specs=[vmem] * 3,
        out_specs=(hbm, hbm, hbm),
        scratch_shapes=[
            pltpu.VMEM(weights.shape, f32),
            dma((2 + chunks,)),
        ],
        compiler_params=pltpu.CompilerParams(vmem_limit_bytes=8 * 2**20),
        name="write_results",
    )(act, grad_sum, input_grad)


def solution(mesh):
    in_specs = (
        P(("groups", "tile"), None, None, None),
        P(),
        P(("groups", "tile"), None, None, None),
        P(("groups", "tile")),
        P(("groups", "tile"), None),
    )
    out_specs = (
        P(("groups", "tile"), None, None, None),
        P("groups", None, None),
        P(("groups", "tile"), None, None, None),
    )
    return jax.shard_map(
        functools.partial(body, mesh.shape["tile"]),
        mesh=mesh,
        in_specs=in_specs,
        out_specs=out_specs,
        check_vma=False,
    )
```
